128 devices in a mesh: section: 2 (over y_hi), ctx: 4 (over z), dp: 8 (over x, core), tp: 2 (over y_lo).
Axes of the slice: x: 4, y: 4 (y_hi: 2, y_lo: 2; y = y_hi * 2 + y_lo), z: 4, core: 2. Of those that a mesh axis runs over, the one named last changes fastest.
Arguments:
- tokens: bfloat16 [8, 2, 512, 1280], P('dp', None, 'ctx'), may hold values from -6 to 6
- ln_gain: float32 [2, 2, 1280], P('section'), may hold values from 0.25 to 1.75
- ln_bias: float32 [2, 2, 1280], P('section'), may hold values from -1.5 to 1.5
- w_qkv: bfloat16 [2, 1280, 3, 1280], P('section', ('ctx', 'dp'), None, 'tp'), may hold values from -0.15625 to 0.15625
- qv_bias: float32 [2, 2, 1280], P('section', None, 'tp'), may hold values from -1.5 to 1.5
- w_out: bfloat16 [2, 1280, 1280], P('section', 'tp', ('ctx', 'dp')), may hold values from -1 to 1
- branch_bias: float32 [2, 2, 1280], P('section'), may hold values from -1.5 to 1.5
- w_up: bfloat16 [2, 1280, 5120], P('section', ('ctx', 'dp'), 'tp'), may hold values from -0.15625 to 0.15625
- up_bias: float32 [2, 5120], P('section', 'tp'), may hold values from -1.5 to 1.5
- w_down: bfloat16 [2, 5120, 1280], P('section', 'tp', ('ctx', 'dp')), may hold values from -0.078125 to 0.078125
- out_grad: bfloat16 [8, 2, 512, 1280], P('dp', None, 'ctx'), may hold values from -6 to 6
Outputs:
- block_out: bfloat16 [8, 2, 512, 1280], P('dp', 'section', 'ctx')
- tokens_grad: bfloat16 [8, 2, 512, 1280], P('dp', 'section', 'ctx')
- ln_gain_grad: float32 [2, 2, 1280], P('section')
- ln_bias_grad: float32 [2, 2, 1280], P('section')
- w_qkv_grad: float32 [2, 1280, 3, 1280], P('section', ('ctx', 'dp'), None, 'tp')
- qv_bias_grad: float32 [2, 2, 1280], P('section', None, 'tp')
- w_out_grad: float32 [2, 1280, 1280], P('section', 'tp', ('ctx', 'dp'))
- branch_bias_grad: float32 [2, 2, 1280], P('section')
- w_up_grad: float32 [2, 1280, 5120], P('section', ('ctx', 'dp'), 'tp')
- up_bias_grad: float32 [2, 5120], P('section', 'tp')
- w_down_grad: float32 [2, 5120, 1280], P('section', 'tp', ('ctx', 'dp'))
The draws below stay inside these ranges and needn't reach their ends.
All inputs are finite; a program needn't handle non-finite values.
Results may differ from the reference program's by a relative error of at most 0.02.
Values may be sent and summed in bfloat16 or wider, within the bound.
A program may use at most 192 MiB of HBM per device.

```python
import jax
import jax.numpy as jnp
from jax import lax

D = 1280
HEADS = 20
HEAD = 64
FF = 5120
MB_LEN = 512
MICRO = 2
SEQS = 8


def with_spikes(entries, own_key, source, target, parts, factor):
    def block_of(dim):
        return (jnp.arange(entries.shape[dim]) // (entries.shape[dim] // parts)).reshape((-1,) + (1,) * (entries.ndim - 1 - dim))

    first = jax.random.permutation(own_key, parts)[block_of(target)]
    second = (block_of(target) + parts // 2) % parts
    return jnp.where((block_of(source) == first) | (block_of(source) == second), factor * entries, entries)


def shard_levels(key, dims, cuts, smallest, largest):
    def one(position, blocks):
        heights = jax.random.uniform(jax.random.fold_in(jax.random.fold_in(key, 6), position), (blocks,), jnp.float32, smallest / len(cuts), largest / len(cuts))
        return jnp.repeat(jnp.exp(heights), dims[position] // blocks).reshape((-1,) + (1,) * (len(dims) - position - 1))

    factor_of = one(*cuts[0])
    for cut in cuts[1:]:
        factor_of = factor_of * one(*cut)
    return factor_of


def gaussian(key, shape, scale, most, cuts=(), held_as=jnp.bfloat16):
    loudness = shard_levels(key, shape, cuts, -0.22, 0.18) if cuts else 1.0
    result = jax.random.normal(key, shape, jnp.float32) * scale * loudness
    return jnp.minimum(jnp.maximum(result, -most), most).astype(held_as)


def bell_draw_with(key, shape, width, bound, pieces, heavy, kind=jnp.bfloat16):
    array = width * jax.random.normal(key, shape, jnp.float32)
    if pieces:
        array = array * shard_levels(key, shape, pieces, -0.22, 0.18)
    return jnp.clip(with_spikes(array, jax.random.fold_in(key, 3), *heavy), -bound, bound).astype(kind)


def setup_inputs(seed: int = 0) -> dict:
    key_list = jax.random.split(jax.random.key(seed), 12)
    return {
        "tokens": bell_draw_with(key_list[0], (SEQS, MICRO, MB_LEN, D), 1.0, 6.0, ((0, 8), (2, 4)), (0, 3, 8, 2.0)),
        "ln_gain": jnp.clip(1.0 + 0.15 * jax.random.normal(key_list[1], (2, 2, D), jnp.float32), 0.25, 1.75),
        "ln_bias": gaussian(key_list[2], (2, 2, D), 0.3, 1.5, ((0, 2),), jnp.float32),
        "w_qkv": gaussian(key_list[3], (2, D, 3, HEADS * HEAD), D ** -0.5, 0.15625, ((0, 2), (1, 32), (3, 2))),
        "qv_bias": gaussian(key_list[4], (2, 2, HEADS * HEAD), 0.3, 1.5, ((0, 2), (2, 2)), jnp.float32),
        "w_out": gaussian(key_list[5], (2, HEADS * HEAD, D), (HEADS * HEAD // 32) ** -0.5, 1.0, ((0, 2), (1, 2), (2, 32))),
        "branch_bias": gaussian(key_list[6], (2, 2, D), 0.3, 1.5, ((0, 2),), jnp.float32),
        "w_up": gaussian(key_list[7], (2, D, FF), D ** -0.5, 0.15625, ((0, 2), (1, 32), (2, 2))),
        "up_bias": gaussian(key_list[8], (2, FF), 0.3, 1.5, ((0, 2), (1, 2)), jnp.float32),
        "w_down": gaussian(key_list[9], (2, FF, D), FF ** -0.5, 0.078125, ((0, 2), (1, 2), (2, 32))),
        "out_grad": bell_draw_with(key_list[10], (SEQS, MICRO, MB_LEN, D), 1.0, 6.0, ((0, 8), (2, 4)), (0, 3, 8, 2.0)),
    }


@jax.custom_vjp
def low(v):
    return lax.optimization_barrier(v.astype(jnp.bfloat16)).astype(jnp.float32)

@jax.custom_vjp
def low_back(v):
    return v

def low_keep(v):
    return (low(v), None)

def low_pass(kept, grad):
    return (grad,)

def back_keep(v):
    return (v, None)

def back_low(kept, grad):
    return (low(grad),)
low.defvjp(low_keep, low_pass)
low_back.defvjp(back_keep, back_low)
EPS = 1e-05
FULL_PRECISION = lax.Precision.HIGHEST

def layer_norm(rows_in, norm_gain, norm_bias):
    row_mean = lax.optimization_barrier(jnp.mean(rows_in, -1, keepdims=True))
    centred = rows_in - row_mean
    spread = lax.optimization_barrier(jnp.mean(centred * centred, -1, keepdims=True))
    return centred * lax.rsqrt(spread + EPS) * norm_gain + norm_bias

def attention(queries, key_heads, value_heads):
    length = queries.shape[0]
    blocks = length // MB_LEN
    query_blocks = queries.reshape(blocks, MB_LEN, HEADS, HEAD)
    starts = jnp.arange(blocks, dtype=jnp.int32) * MB_LEN
    key_pos = jnp.arange(length, dtype=jnp.int32)

    def one_block(pair):
        query_block, start = pair
        scores = low_back(HEAD ** (-0.5) * jnp.einsum('qhe,khe->hqk', query_block, key_heads, precision=FULL_PRECISION))
        query_pos = start + jnp.arange(MB_LEN, dtype=jnp.int32)
        allowed = key_pos[None, :] <= query_pos[:, None]
        probs = jax.nn.softmax(jnp.where(allowed[None], scores, -jnp.inf), axis=-1)
        return jnp.einsum('hqk,khe->qhe', probs, value_heads, precision=FULL_PRECISION)
    attended = lax.map(jax.checkpoint(one_block), (query_blocks, starts))
    return attended.reshape(length, HEADS * HEAD)

def layer(rows_in, params, layer_index):
    ln_gain, ln_bias, w_qkv, qv_bias, w_out, branch_bias, w_up, up_bias, w_down = params
    normed = low(layer_norm(rows_in, ln_gain[layer_index, 0], ln_bias[layer_index, 0]))
    projected = jnp.einsum('ld,dkf->lkf', normed, w_qkv[layer_index], precision=FULL_PRECISION)
    queries = low(low_back(projected[:, 0] + qv_bias[layer_index, 0]))
    key_heads = low(low_back(projected[:, 1]))
    value_heads = low(low_back(projected[:, 2] + qv_bias[layer_index, 1]))
    head_shape = (rows_in.shape[0], HEADS, HEAD)
    attended = low(low_back(attention(queries.reshape(head_shape), key_heads.reshape(head_shape), value_heads.reshape(head_shape))))
    mixed = rows_in + low_back(jnp.dot(attended, w_out[layer_index], precision=FULL_PRECISION) + branch_bias[layer_index, 0])
    second = low(layer_norm(mixed, ln_gain[layer_index, 1], ln_bias[layer_index, 1]))
    hidden_pre = low_back(jnp.dot(second, w_up[layer_index], precision=FULL_PRECISION) + up_bias[layer_index])
    hidden = low(jax.nn.gelu(hidden_pre, approximate=True))
    return mixed + jnp.dot(hidden, w_down[layer_index], precision=FULL_PRECISION) + branch_bias[layer_index, 1]

def two_layers(rows_in, params):
    first = layer(rows_in, params, 0)
    return layer(low(low_back(first)), params, 1)

def reference(tokens, ln_gain, ln_bias, w_qkv, qv_bias, w_out, branch_bias, w_up, up_bias, w_down, out_grad):
    params = tuple((member.astype(jnp.float32) for member in (ln_gain, ln_bias, w_qkv, qv_bias, w_out, branch_bias, w_up, up_bias, w_down)))
    length = MICRO * MB_LEN
    inputs = tokens.astype(jnp.float32).reshape(SEQS, length, D)

    def forward(seq_inputs, weights):
        return lax.map(jax.checkpoint(lambda one_seq: two_layers(one_seq, weights)), seq_inputs)
    outputs, pull = jax.vjp(forward, inputs, params)
    input_grad, weight_grads = pull(out_grad.astype(jnp.float32).reshape(SEQS, length, D))
    full_shape = tokens.shape
    block_out = outputs.reshape(full_shape).astype(jnp.bfloat16)
    tokens_grad = input_grad.reshape(full_shape).astype(jnp.bfloat16)
    return (block_out, tokens_grad, weight_grads[0], weight_grads[1], weight_grads[2], weight_grads[3], weight_grads[4], weight_grads[5], weight_grads[6], weight_grads[7], weight_grads[8])
```

```python
import jax
import jax.numpy as jnp
from jax import lax
from jax.experimental import pallas as pl
from jax.experimental.pallas import tpu as pltpu
from jax.sharding import PartitionSpec as P

MESH = pl.DeviceIdType.MESH
F32 = jnp.float32
BF16 = jnp.bfloat16
D = 1280
HEAD = 64
HEADS = 5
ROWS = 64
KV, QO, UP, DOWN, COLS = (0, 640, 1280, 2560, 3840)
OWN = 40
CHIP = 80
HALF = 1920
CUT = 1024
EPS = 1e-05
NEG = -1e30
MIB = 2**20


class Place:
    def __init__(self):
        self.s = lax.axis_index("section")
        self.z = lax.axis_index("ctx")
        self.dp = lax.axis_index("dp")
        self.t = lax.axis_index("tp")
        self.x = self.dp // 2
        self.c = self.dp % 2

    def core(self):
        return (self.s, self.z, self.x * 2 + 1 - self.c, self.t)

    def pair(self):
        return (self.s, self.z, self.dp, 1 - self.t)

    def other(self):
        return (1 - self.s, self.z, self.dp, self.t)

    def away(self, dz, dx):
        return (self.s, (self.z + dz + 4) % 4, (self.x + dx + 4) % 4 * 2 + self.c, self.t)

    def at(self, s, seq, t):
        return (s, self.z, self.x * 2 + seq, t)


def send(source, target, sems, device):
    copy = pltpu.make_async_remote_copy(
        src_ref=source,
        dst_ref=target,
        send_sem=sems[0],
        recv_sem=sems[1],
        device_id=device,
        device_id_type=MESH,
    )
    copy.start()
    return copy


def greet(devices):
    barrier = pltpu.get_barrier_semaphore()
    for device in devices:
        pl.semaphore_signal(barrier, inc=1, device_id=device, device_id_type=MESH)
    return barrier


def in_turn(*stages):
    live = list(stages)
    while live:
        for stage in list(live):
            if next(stage, "end") == "end":
                live.remove(stage)


def mm(a, b):
    return lax.dot_general(a, b, (((1,), (0,)), ((), ())), preferred_element_type=F32)


def mm_nt(a, b):
    return lax.dot_general(a, b, (((1,), (1,)), ((), ())), preferred_element_type=F32)


def mm_tn(a, b):
    return lax.dot_general(a, b, (((0,), (0,)), ((), ())), preferred_element_type=F32)


def gather_kernel(shard, w, peer, core_sems, send_sems, recv_sems):
    me = Place()
    devices = [me.core()] + [me.away(dz, dx) for dz, dx in ((1, 0), (-1, 0), (0, 1), (0, -1))]
    pl.semaphore_wait(greet(devices), 5)
    swap = send(shard.at[1 - me.c], peer, (core_sems.at[0], core_sems.at[1]), me.core())
    swap.wait()
    row = pl.multiple_of((me.z * 4 + me.x) * CHIP, 16)
    for start in range(0, COLS, 640):
        columns = slice(start, start + 640)
        mine = shard[me.c, :, columns]
        theirs = peer[:, columns]
        lower = jnp.where(me.c == 0, mine, theirs)
        upper = jnp.where(me.c == 0, theirs, mine)
        w[pl.ds(row, CHIP), columns] = jnp.concatenate((lower, upper), 0).astype(BF16)

    def region(half, i, j, part):
        dz, dx = (j, i) if half == 0 else (i, j)
        top = ((me.z + dz + 4) % 4 * 4 + (me.x + dx + 4) % 4) * CHIP
        left = half * HALF + (CUT if part == 1 else 0)
        width = HALF if part is None else (CUT, HALF - CUT)[part]
        return w.at[pl.ds(pl.multiple_of(top, 16), CHIP), pl.ds(left, width)]

    def step(half, i, j, part, first, by, group, kind):
        along = (0, by) if (half == 0) == first else (by, 0)
        ref = region(half, i, j, part)
        sems = (send_sems.at[half, group, kind], recv_sems.at[half, group, kind])
        return send(ref, ref, sems, me.away(*along))

    flying = {}

    def go(half, i, j, part, first, by, group, kind):
        flying[half, group, kind] = step(half, i, j, part, first, by, group, kind)

    def across(half, group, i):
        go(half, i, 0, None, False, 1, group, 0)
        go(half, i, 0, None, False, -1, group, 1)

    def landed(half, group, kind):
        flying[half, group, kind].wait_recv()

    for half in (0, 1):
        go(half, 0, 0, None, True, 1, 0, 0)
        go(half, 0, 0, None, True, -1, 0, 1)
    for half in (0, 1):
        across(half, 1, 0)
    for half in (0, 1):
        landed(half, 0, 0)
        go(half, -1, 0, 0, True, 1, 0, 2)
        across(half, 2, -1)
        landed(half, 0, 1)
        go(half, 1, 0, 1, True, -1, 0, 3)
        across(half, 3, 1)
    for half in (0, 1):
        landed(half, 1, 0)
        go(half, 0, -1, 0, False, 1, 1, 2)
        landed(half, 1, 1)
        go(half, 0, 1, 1, False, -1, 1, 3)
    for half in (0, 1):
        landed(half, 0, 2)
        landed(half, 0, 3)
        across(half, 4, 2)
    for group, i in ((2, -1), (3, 1), (4, 2)):
        for half in (0, 1):
            landed(half, group, 0)
            go(half, i, -1, 0, False, 1, group, 2)
            landed(half, group, 1)
            go(half, i, 1, 1, False, -1, group, 3)
    for group in (1, 2, 3, 4):
        for half in (0, 1):
            landed(half, group, 2)
            landed(half, group, 3)
    for copy in flying.values():
        copy.wait_send()


def scatter_kernel(
    grads,
    home_sum,
    quarter_sum,
    out_rows,
    grad_rows,
    shares,
    home_total,
    quarter_total,
    out_block,
    grad_block,
    landing,
    passing,
    first_sums,
    reduced,
    from_core,
    small,
    small_in,
    send_sems,
    recv_sems,
    core_sems,
    small_send,
    small_recv,
    rows_send,
    rows_recv,
):
    me = Place()
    devices = [me.core(), me.pair()]
    devices += [me.away(dz, dx) for dz, dx in ((1, 0), (2, 0), (3, 0), (0, 1), (0, 2), (0, 3))]
    barrier = greet(devices)
    kinds = ((1, out_rows, out_block), (0, grad_rows, grad_block))
    for origin, _, _ in kinds:
        for seq in (0, 1):
            itself = (me.s == origin) & (me.c == seq) & (me.t == me.s)

            @pl.when(jnp.logical_not(itself))
            def _():
                pl.semaphore_signal(
                    barrier, inc=1, device_id=me.at(origin, seq, me.s), device_id_type=MESH
                )

    pl.semaphore_wait(barrier, 8 + 4 - (me.t == me.s).astype(jnp.int32))

    def rows_copies(kind, act):
        origin, source, target = kinds[kind]

        @pl.when(me.s == origin)
        def _():
            for seq in (0, 1):
                for t in (0, 1):
                    itself = (me.t == me.s) & (me.c == seq) & (me.t == t)
                    place = target.at[pl.ds(pl.multiple_of(me.c * ROWS, ROWS), ROWS)]

                    @pl.when(jnp.logical_not(itself))
                    def _():
                        copy = pltpu.make_async_remote_copy(
                            src_ref=source.at[seq],
                            dst_ref=place,
                            send_sem=rows_send.at[kind, seq, t],
                            recv_sem=rows_recv.at[kind, me.c],
                            device_id=me.at(me.t, seq, t),
                            device_id_type=MESH,
                        )
                        if act == "start":
                            copy.start()
                        else:
                            copy.wait_send()

                    if act == "start":

                        @pl.when(itself)
                        def _():
                            place[...] = source[seq]

    def rows_arrive(kind):
        origin, source, target = kinds[kind]
        for seq in (0, 1):
            itself = (me.s == origin) & (me.c == seq) & (me.t == me.s)

            @pl.when(jnp.logical_not(itself))
            def _():
                pltpu.make_async_remote_copy(
                    src_ref=source.at[0],
                    dst_ref=target.at[pl.ds(seq * ROWS, ROWS)],
                    send_sem=rows_send.at[kind, 0, 0],
                    recv_sem=rows_recv.at[kind, seq],
                    device_id=me.core(),
                    device_id_type=MESH,
                ).wait_recv()

    parts = ((0, CUT), (CUT, HALF - CUT))
    flying = {}

    def go(half, group, kind, source, slot, part, by):
        first = group != 4
        along = (by, 0) if (half == 0) == first else (0, by)
        target = landing.at[half, group, slot, :, pl.ds(*parts[part])]
        sems = (send_sems.at[half, group, kind], recv_sems.at[half, group, kind])
        flying[half, group, kind] = send(source, target, sems, me.away(*along))

    def piece(half, group, j, part):
        left, width = parts[part]
        if group == 4:
            return first_sums.at[half, j % 4, :, pl.ds(left, width)]
        dz, dx = (j, group) if half == 0 else (group, j)
        top = ((me.z + dz + 4) % 4 * 4 + (me.x + dx + 4) % 4) * CHIP
        return grads.at[pl.ds(pl.multiple_of(top, 16), CHIP), pl.ds(half * HALF + left, width)]

    def begin(half, group):
        go(half, group, 0, piece(half, group, 2, 0), 0, 0, 1)
        go(half, group, 1, piece(half, group, 2, 1), 0, 1, -1)
        go(half, group, 2, piece(half, group, 1, 1), 1, 1, 1)
        go(half, group, 3, piece(half, group, -1, 0), 2, 0, -1)

    def pass_on(half, group):
        for kind, part, j, by, slot in ((0, 0, 1, 1, 1), (1, 1, -1, -1, 2)):
            flying[half, group, kind].wait_recv()
            columns = slice(parts[part][0], sum(parts[part]))
            own = piece(half, group, j, part)[...].astype(F32)
            arrived = landing[half, group, 0, :, columns].astype(F32)
            passing[half, group, :, columns] = (own + arrived).astype(BF16)
            source = passing.at[half, group, :, pl.ds(*parts[part])]
            go(half, group, 4 + kind, source, slot, part, by)

    def finish(half, group):
        for kind in (2, 3, 4, 5):
            flying[half, group, kind].wait_recv()
        for part in (0, 1):
            columns = slice(parts[part][0], sum(parts[part]))
            total = (
                piece(half, group, 0, part)[...].astype(F32)
                + landing[half, group, 1, :, columns].astype(F32)
                + landing[half, group, 2, :, columns].astype(F32)
            )
            if group == 4:
                left = half * HALF + parts[part][0]
                reduced[:, left : left + parts[part][1]] = total
            else:
                first_sums[half, group, :, columns] = total.astype(BF16)

    rows_copies(0, "start")
    rows_copies(1, "start")
    for group in (2, 1, 3):
        for half in (0, 1):
            begin(half, group)

    small[0, 0:8, :] = home_sum[...]
    small[0, 8:16, :] = quarter_sum[...]
    small_flying = []

    def small_step(step, rows, devices):
        sent = []
        for index, device in enumerate(devices):
            sems = (small_send.at[step, index], small_recv.at[step, index])
            sent.append(
                send(small.at[step, pl.ds(0, rows)], small_in.at[step, index, pl.ds(0, rows)], sems, device)
            )
        small_flying.extend(sent)
        yield
        for copy in sent:
            copy.wait_recv()
        total = small[step, 0:rows, :]
        for index in range(len(devices)):
            total = total + small_in[step, index, 0:rows, :]
        small[step + 1, 0:rows, :] = total
        if rows == 8:
            small[step + 1, 8:16, :] = small[step, 8:16, :]

    def small_steps():
        yield from small_step(0, 8, [me.core()])
        yield from small_step(1, 8, [me.pair()])
        yield from small_step(2, 16, [me.away(0, dx) for dx in (1, 2, 3)])
        yield from small_step(3, 16, [me.away(dz, 0) for dz in (1, 2, 3)])

    smalls = small_steps()
    next(smalls)
    for group in (0,):
        for half in (0, 1):
            begin(half, group)
    for group in (2, 1, 3):
        for half in (0, 1):
            pass_on(half, group)
        next(smalls, None)
    for half in (0, 1):
        pass_on(half, 0)
    for group in (2, 1, 3):
        for half in (0, 1):
            finish(half, group)
    for half in (0, 1):
        begin(half, 4)
    for half in (0, 1):
        finish(half, 0)
    for half in (0, 1):
        pass_on(half, 4)
    next(smalls, None)
    home_total[...] = small[4, 0:8, :]
    quarter_total[me.c] = small[4, 8:16, :]
    sems = (core_sems.at[2], core_sems.at[3])
    vector_swap = send(small.at[4, pl.ds(8, 8)], quarter_total.at[me.c], sems, me.core())
    for half in (0, 1):
        finish(half, 4)
    theirs = pl.ds(pl.multiple_of((1 - me.c) * OWN, 8), OWN)
    sems = (core_sems.at[0], core_sems.at[1])
    swap = send(reduced.at[theirs], shares.at[me.c], sems, me.core())
    shares[me.c] = reduced[pl.ds(pl.multiple_of(me.c * OWN, 8), OWN), :]
    rows_arrive(0)
    rows_arrive(1)
    swap.wait()
    vector_swap.wait()
    for copy in flying.values():
        copy.wait_send()
    for copy in small_flying:
        copy.wait_send()
    rows_copies(0, "wait")
    rows_copies(1, "wait")


def layers_kernel(
    tokens,
    out_grad,
    w,
    ln_gain,
    ln_bias,
    kv_bias,
    qo_bias,
    branch_bias,
    up_bias,
    grads,
    out_rows,
    grad_rows,
    home_sum,
    quarter_sum,
    x_in,
    g_in,
    a_all,
    c_all,
    g_all,
    ga_all,
    q_pad,
    kv_all,
    probs_one,
    probs_two,
    o_all,
    u_all,
    hidden,
    du_all,
    go_pad,
    dqkv,
    dkv_part,
    dkv_in,
    dkv_pass,
    part,
    core_in,
    pair_out,
    pair_in,
    normed,
    recips,
    turned,
    sems_s,
    sems_r,
    hop_sems,
):
    me = Place()
    devices = [me.core(), me.pair(), me.away(1, 0), me.away(-1, 0), me.other()]
    pl.semaphore_wait(greet(devices), 5)
    counter = {0: 0, 1: 0}

    def new_sems(seq):
        index = counter[seq]
        counter[seq] = index + 1
        return (sems_s.at[seq, index], sems_r.at[seq, index])

    flying = []

    def fly(source, target, seq, device):
        copy = send(source, target, new_sems(seq), device)
        flying.append(copy)
        return copy

    lanes = lax.broadcasted_iota(jnp.int32, (256, 640), 1) % 128
    low_lanes = lanes < HEAD

    def first_rows(section, whole, rows_in):
        @pl.when(me.s == section)
        def _():
            mine = pl.ds(pl.multiple_of(me.c * ROWS, ROWS), ROWS)
            theirs = pl.ds(pl.multiple_of((1 - me.c) * ROWS, ROWS), ROWS)
            sems = (hop_sems.at[0, section, me.c], hop_sems.at[1, section, me.c])
            copy = send(whole.at[me.t, theirs], rows_in.at[me.c], sems, me.core())
            rows_in[me.c] = whole[me.t, mine, :]
            copy.wait_send()

    def rows_ready(section, whole, rows_in, seq):
        @pl.when(jnp.logical_not((me.s == section) & (me.c == seq)))
        def _():
            pltpu.make_async_remote_copy(
                src_ref=rows_in.at[seq],
                dst_ref=rows_in.at[seq],
                send_sem=hop_sems.at[0, section, seq],
                recv_sem=hop_sems.at[1, section, seq],
                device_id=me.core(),
                device_id_type=MESH,
            ).wait_recv()

    def hop(section, rows_out, rows_in, seq):
        @pl.when(me.s == section)
        def _():
            sems = (hop_sems.at[2, section, seq], hop_sems.at[1, section, seq])
            send(rows_out.at[seq], rows_in.at[seq], sems, me.other()).wait_send()

    def spread(rows, seq):
        own = rows.at[seq, me.t, me.c]
        pair = fly(own, own, seq, me.pair())
        core = fly(own, own, seq, me.core())
        yield
        pair.wait_recv()
        arrived = rows.at[seq, 1 - me.t, me.c]
        further = fly(arrived, arrived, seq, me.core())
        yield
        core.wait_recv()
        further.wait_recv()

    parts_flying = {0: [], 1: []}

    def before_part(seq):
        for copy in parts_flying[seq]:
            copy.wait_send()
        parts_flying[seq] = []

    def collect(which, seq):
        arriving = core_in.at[seq, which]
        core = send(part.at[seq, :, 1 - me.c], arriving, new_sems(seq), me.core())
        parts_flying[seq].append(core)
        yield
        core.wait_recv()
        theirs = part[seq, 1 - me.t, me.c].astype(F32) + core_in[seq, which, 1 - me.t].astype(F32)
        pair_out[seq, which] = theirs.astype(BF16)
        pair = fly(pair_out.at[seq, which], pair_in.at[seq, which], seq, me.pair())
        mine = part[seq, me.t, me.c].astype(F32) + core_in[seq, which, me.t].astype(F32)
        yield
        pair.wait_recv()
        return mine + pair_in[seq, which].astype(F32)

    def norm(rows, which, seq, target):
        centred = rows - jnp.mean(rows, -1, keepdims=True)
        recip = lax.rsqrt(jnp.mean(centred * centred, -1, keepdims=True) + EPS)
        units = centred * recip
        normed[seq, which] = units
        recips[seq, which] = recip
        out = units * ln_gain[which : which + 1, :] + ln_bias[which : which + 1, :]
        target[seq, me.t, me.c] = out.astype(BF16)

    def norm_back(grad, which, seq):
        units = normed[seq, which]
        scaled = grad * ln_gain[which : which + 1, :]
        inner = (
            scaled
            - jnp.mean(scaled, -1, keepdims=True)
            - units * jnp.mean(scaled * units, -1, keepdims=True)
        )
        home_sum[which : which + 1, :] += jnp.sum(grad * units, 0, keepdims=True)
        home_sum[2 + which : 3 + which, :] += jnp.sum(grad, 0, keepdims=True)
        return inner * recips[seq, which]

    def tiled(count, body):
        def one(n, carry):
            body(pl.multiple_of(n * 256, 256))
            return carry

        lax.fori_loop(0, count, one, 0)

    def back_through(rows, left, width, seq):
        def tile(n):
            out = mm_nt(rows, w[pl.ds(n, 256), left : left + width])
            part[seq, :, :, :, pl.ds(n, 256)] = out.reshape(2, 2, ROWS, 256).astype(BF16)

        tiled(5, tile)

    def causal(width):
        query = me.z * 128 + lax.broadcasted_iota(jnp.int32, (128, width), 0)
        key = lax.broadcasted_iota(jnp.int32, (128, width), 1) - (width - 512)
        return key <= query

    def forward(seq):
        rows_ready(0, tokens, x_in, seq)
        rows = x_in[seq].astype(F32)
        norm(rows, 0, seq, a_all)
        yield from spread(a_all, seq)
        a = a_all[seq].reshape(256, D)
        pairs = (mm(a, w[:, KV:QO]) + kv_bias[me.c]).astype(BF16)
        for head in range(HEADS):
            kv_all[seq, head, :, me.z] = pairs[:, head * 128 : head * 128 + 128].reshape(2, 128, 128)
        own = kv_all.at[seq, :, :, me.z]
        up = fly(own, own, seq, me.away(1, 0))
        down = fly(own, own, seq, me.away(-1, 0))
        queries = jnp.where(low_lanes, mm(a, w[:, QO:UP]) + qo_bias[me.c], 0.0)
        queries = (queries.astype(BF16).astype(F32) * HEAD**-0.5).astype(BF16)
        for head in range(HEADS):
            q_pad[seq, head] = queries[:, head * 128 : head * 128 + 128]
        yield
        up.wait_recv()
        arrived = kv_all.at[seq, :, 0, (me.z + 3) % 4]
        up = fly(arrived, arrived, seq, me.away(1, 0))
        down.wait_recv()
        arrived = kv_all.at[seq, :, 1, (me.z + 1) % 4]
        down = fly(arrived, arrived, seq, me.away(-1, 0))
        yield
        up.wait_recv()
        down.wait_recv()

        def one_head(head, carry):
            pairs = kv_all[seq, head].reshape(1024, 128)
            columns = pl.ds(pl.multiple_of(head * 128, 128), 128)
            high = lax.broadcasted_iota(jnp.int32, (128, 128), 1) >= HEAD
            for block, probs, width in ((0, probs_one, 512), (1, probs_two, 1024)):
                top = block * 128
                scores = mm_nt(q_pad[seq, head, top : top + 128, :], pairs[:width])
                scores = jnp.where(causal(width), scores, NEG)
                weights = jnp.exp(scores - jnp.max(scores, -1, keepdims=True))
                weights = weights / jnp.sum(weights, -1, keepdims=True)
                weights = weights.astype(BF16)
                probs[seq, head] = weights
                out = jnp.where(high, mm(weights, pairs[:width]), 0.0)
                o_all[seq, top : top + 128, columns] = out.astype(BF16)
            return carry

        lax.fori_loop(0, HEADS, one_head, 0)
        back_through(o_all[seq], QO, 640, seq)
        total = yield from collect(0, seq)
        rows = rows + total + branch_bias[0:1, :]
        norm(rows, 1, seq, c_all)
        yield from spread(c_all, seq)

        def up_tile(n):
            columns = pl.ds(n, 256)
            pre = mm(c_all[seq].reshape(256, D), w[:, pl.ds(UP + n, 256)]) + up_bias[me.c, :, columns]
            u_all[seq, :, columns] = pre
            hidden[seq, :, columns] = jax.nn.gelu(pre, approximate=True).astype(BF16)

        tiled(5, up_tile)
        before_part(seq)
        back_through(hidden[seq], DOWN, 1280, seq)
        total = yield from collect(1, seq)
        rows = rows + total + branch_bias[1:2, :]
        out_rows[seq] = rows.astype(BF16)
        hop(0, out_rows, x_in, seq)

    def backward(seq):
        rows_ready(1, out_grad, g_in, seq)
        rows = g_in[seq]
        g_all[seq, me.t, me.c] = rows
        rows = rows.astype(F32)
        home_sum[5:6, :] += jnp.sum(rows, 0, keepdims=True)
        yield from spread(g_all, seq)

        def down_tile(n):
            columns = pl.ds(n, 256)
            grad = mm(g_all[seq].reshape(256, D), w[:, pl.ds(DOWN + n, 256)])
            pre = u_all[seq, :, columns]
            scale = 0.7978845608028654
            curve = jnp.tanh(scale * (pre + 0.044715 * (pre * pre * pre)))
            slope = 0.5 * (1.0 + curve) + 0.5 * pre * (1.0 - curve * curve) * (
                scale * (1.0 + 3 * 0.044715 * (pre * pre))
            )
            grad = (grad * slope).astype(BF16)
            du_all[seq, :, columns] = grad
            quarter_sum[1:2, columns] += jnp.sum(grad.astype(F32), 0, keepdims=True)

        tiled(5, down_tile)
        before_part(seq)
        back_through(du_all[seq], UP, 1280, seq)
        total = yield from collect(2, seq)
        rows = rows + norm_back(total, 1, seq)
        low = rows.astype(BF16)
        ga_all[seq, me.t, me.c] = low
        home_sum[4:5, :] += jnp.sum(low.astype(F32), 0, keepdims=True)
        yield from spread(ga_all, seq)
        grad = mm(ga_all[seq].reshape(256, D), w[:, QO:UP])
        go_pad[seq] = jnp.where(low_lanes, 0.0, grad).astype(BF16)

        def one_head(head, carry):
            pairs = kv_all[seq, head].reshape(1024, 128)
            columns = pl.ds(pl.multiple_of(head * 128, 128), 128)
            low_half = lax.broadcasted_iota(jnp.int32, (128, 128), 1) < HEAD
            out_grads = go_pad[seq, :, columns]
            queries = q_pad[seq, head]
            score_grads = []
            weights = []
            for block, probs, width in ((0, probs_one, 512), (1, probs_two, 1024)):
                top = block * 128
                low = probs[seq, head]
                pulled = low.astype(F32) * mm_nt(out_grads[top : top + 128], pairs[:width])
                delta = jnp.sum(pulled, -1, keepdims=True)
                grad = (pulled - low.astype(F32) * delta).astype(BF16)
                query_grad = mm(grad, pairs[:width]) * HEAD**-0.5
                place = pl.ds(pl.multiple_of(QO + head * 128, 128), 128)
                dqkv[seq, top : top + 128, place] = jnp.where(low_half, query_grad, 0.0).astype(BF16)
                score_grads.append(grad)
                weights.append(low)
            early = mm_tn(jnp.concatenate((score_grads[0], score_grads[1][:, :512]), 0), queries)
            early += mm_tn(jnp.concatenate((weights[0], weights[1][:, :512]), 0), out_grads)
            late = mm_tn(score_grads[1][:, 512:], queries[128:])
            late += mm_tn(weights[1][:, 512:], out_grads[128:])
            dkv_part[seq, head, 0] = early.reshape(4, 128, 128).astype(BF16)
            dkv_part[seq, head, 1] = late.reshape(4, 128, 128).astype(BF16)
            return carry

        lax.fori_loop(0, HEADS, one_head, 0)
        far, right, left = ((me.z + 2) % 4, (me.z + 1) % 4, (me.z + 3) % 4)
        far_up = fly(dkv_part.at[seq, :, 0, far], dkv_in.at[seq, 0, :, 0], seq, me.away(1, 0))
        far_down = fly(dkv_part.at[seq, :, 1, far], dkv_in.at[seq, 0, :, 1], seq, me.away(-1, 0))
        up_own = fly(dkv_part.at[seq, :, 1, right], dkv_in.at[seq, 1, :, 1], seq, me.away(1, 0))
        down_own = fly(dkv_part.at[seq, :, 0, left], dkv_in.at[seq, 2, :, 0], seq, me.away(-1, 0))
        yield
        far_up.wait_recv()
        total = dkv_part[seq, :, 0, right].astype(F32) + dkv_in[seq, 0, :, 0].astype(F32)
        dkv_pass[seq, :, 0] = total.astype(BF16)
        up_sum = fly(dkv_pass.at[seq, :, 0], dkv_in.at[seq, 1, :, 0], seq, me.away(1, 0))
        far_down.wait_recv()
        total = dkv_part[seq, :, 1, left].astype(F32) + dkv_in[seq, 0, :, 1].astype(F32)
        dkv_pass[seq, :, 1] = total.astype(BF16)
        down_sum = fly(dkv_pass.at[seq, :, 1], dkv_in.at[seq, 2, :, 1], seq, me.away(-1, 0))
        yield
        for copy in (up_own, down_own, up_sum, down_sum):
            copy.wait_recv()
        for head in range(HEADS):
            total = (
                dkv_part[seq, head, :, me.z].astype(F32)
                + dkv_in[seq, 1, head].astype(F32)
                + dkv_in[seq, 2, head].astype(F32)
            )
            dqkv[seq, :, head * 128 : head * 128 + 128] = total.reshape(256, 128).astype(BF16)
        before_part(seq)
        back_through(dqkv[seq], KV, 1280, seq)
        yield from collect_last(seq, rows)

    def collect_last(seq, rows):
        total = yield from collect(3, seq)
        rows = rows + norm_back(total, 0, seq)
        grad_rows[seq] = rows.astype(BF16)
        hop(1, grad_rows, g_in, seq)

    home_sum[...] = jnp.zeros_like(home_sum)
    quarter_sum[...] = jnp.zeros_like(quarter_sum)
    first_rows(0, tokens, x_in)
    first_rows(1, out_grad, g_in)
    in_turn(forward(0), forward(1))
    in_turn(backward(0), backward(1))

    def grad_tiles(rows, columns, other, left, count, more):
        turned[...] = rows[...].reshape(512, D).T

        def tile(n):
            out = mm(turned[...], other[:, :, pl.ds(columns + n, 256)].reshape(512, 256))
            place = pl.ds(left + n, 256)
            if more:
                out = out + grads[:, place].astype(F32)
            grads[:, place] = out.astype(BF16)

        tiled(count, tile)

    grad_tiles(g_all, 0, hidden, DOWN, 5, False)
    grad_tiles(c_all, 0, du_all, UP, 5, False)
    grad_tiles(a_all, 0, dqkv, KV, 5, False)
    turned[...] = ga_all[...].reshape(512, D).T
    for start in (0, 256, 512):
        width = min(256, 640 - start)
        columns = slice(QO + start, QO + start + width)
        out = mm(turned[...], o_all[:, :, start : start + width].reshape(512, width))
        grads[:, columns] = (out + grads[:, columns].astype(F32)).astype(BF16)
    column_sum = jnp.sum(dqkv[...].astype(F32), axis=(0, 1))
    quarter_sum[0:1, :] += column_sum.reshape(1, D)
    for copy in flying:
        copy.wait_send()
    before_part(0)
    before_part(1)


def vmem(shape, kind):
    return pltpu.VMEM(shape, kind)


def call(kernel, name, operands, outs, scratch, collective_id, flops):
    whole = pl.BlockSpec(memory_space=pltpu.VMEM)
    moved = sum(a.size * a.dtype.itemsize for a in operands)
    return pl.pallas_call(
        kernel,
        name=name,
        out_shape=[jax.ShapeDtypeStruct(shape, kind) for shape, kind in outs],
        in_specs=[whole] * len(operands),
        out_specs=[whole] * len(outs),
        scratch_shapes=scratch,
        cost_estimate=pl.CostEstimate(flops=flops, bytes_accessed=moved, transcendentals=0),
        compiler_params=pltpu.CompilerParams(
            collective_id=collective_id, has_side_effects=True, vmem_limit_bytes=62 * MIB
        ),
    )(*operands)


def per_device(
    tokens, ln_gain, ln_bias, w_qkv, qv_bias, w_out, branch_bias, w_up, up_bias, w_down, out_grad
):
    dma = pltpu.SemaphoreType.DMA
    halves = w_qkv[0].reshape(OWN, 3, 2 * HEADS, HEAD)
    out_turned = w_out[0].T.reshape(OWN, 2 * HEADS, HEAD)
    shard = jnp.concatenate(
        (
            jnp.concatenate((halves[:, 1], halves[:, 2]), -1).reshape(OWN, 2, 640),
            jnp.concatenate((halves[:, 0], out_turned), -1).reshape(OWN, 2, 640),
            w_up[0].reshape(OWN, 2, D),
            w_down[0].T.reshape(OWN, 2, D),
        ),
        -1,
    )
    shard = shard.transpose(1, 0, 2).astype(F32)
    biases = qv_bias[0].reshape(2, 2, HEADS, HEAD)
    none = jnp.zeros((2, HEADS, HEAD), F32)
    kv_bias = jnp.concatenate((none, biases[1]), -1).reshape(2, 1, 640)
    qo_bias = jnp.concatenate((biases[0], none), -1).reshape(2, 1, 640)

    (w,) = call(
        gather_kernel,
        "gather_weights",
        [shard],
        [((D, COLS), BF16)],
        [vmem((OWN, COLS), F32), dma((2,)), dma((2, 5, 4)), dma((2, 5, 4))],
        0,
        0,
    )
    grads, out_rows, grad_rows, home_sum, quarter_sum = call(
        layers_kernel,
        "layers",
        [
            tokens[0],
            out_grad[0],
            w,
            ln_gain[0],
            ln_bias[0],
            kv_bias,
            qo_bias,
            branch_bias[0],
            up_bias[0].reshape(2, 1, D),
        ],
        [
            ((D, COLS), BF16),
            ((2, ROWS, D), BF16),
            ((2, ROWS, D), BF16),
            ((8, D), F32),
            ((8, D), F32),
        ],
        [
            vmem((2, ROWS, D), BF16),
            vmem((2, ROWS, D), BF16),
            vmem((2, 2, 2, ROWS, D), BF16),
            vmem((2, 2, 2, ROWS, D), BF16),
            vmem((2, 2, 2, ROWS, D), BF16),
            vmem((2, 2, 2, ROWS, D), BF16),
            vmem((2, HEADS, 256, 128), BF16),
            vmem((2, HEADS, 2, 4, 128, 128), BF16),
            vmem((2, HEADS, 128, 512), BF16),
            vmem((2, HEADS, 128, 1024), BF16),
            vmem((2, 256, 640), BF16),
            vmem((2, 256, D), F32),
            vmem((2, 256, D), BF16),
            vmem((2, 256, D), BF16),
            vmem((2, 256, 640), BF16),
            vmem((2, 256, D), BF16),
            vmem((2, HEADS, 2, 4, 128, 128), BF16),
            vmem((2, 3, HEADS, 2, 128, 128), BF16),
            vmem((2, HEADS, 2, 128, 128), BF16),
            vmem((2, 2, 2, ROWS, D), BF16),
            vmem((2, 4, 2, ROWS, D), BF16),
            vmem((2, 4, ROWS, D), BF16),
            vmem((2, 4, ROWS, D), BF16),
            vmem((2, 2, ROWS, D), F32),
            vmem((2, 2, ROWS, 1), F32),
            vmem((D, 512), BF16),
            dma((2, 32)),
            dma((2, 32)),
            dma((3, 2, 2)),
        ],
        1,
        2 * 512 * D * COLS * 3,
    )
    shares, home_total, quarter_total, out_block, grad_block = call(
        scatter_kernel,
        "scatter_gradients",
        [grads, home_sum, quarter_sum, out_rows, grad_rows],
        [
            ((2, OWN, COLS), F32),
            ((8, D), F32),
            ((2, 8, D), F32),
            ((2 * ROWS, D), BF16),
            ((2 * ROWS, D), BF16),
        ],
        [
            vmem((2, 5, 3, CHIP, HALF), BF16),
            vmem((2, 5, CHIP, HALF), BF16),
            vmem((2, 4, CHIP, HALF), BF16),
            vmem((CHIP, COLS), F32),
            vmem((8, D), F32),
            vmem((5, 16, D), F32),
            vmem((4, 3, 16, D), F32),
            dma((2, 5, 6)),
            dma((2, 5, 6)),
            dma((4,)),
            dma((4, 3)),
            dma((4, 3)),
            dma((2, 2, 2)),
            dma((2, 2)),
        ],
        2,
        0,
    )
    shares = shares.transpose(1, 0, 2)
    pairs = shares[:, :, KV:QO].reshape(OWN, 2 * HEADS, 2, HEAD)
    others = shares[:, :, QO:UP].reshape(OWN, 2 * HEADS, 2, HEAD)
    qkv_grad = jnp.stack((others[:, :, 0], pairs[:, :, 0], pairs[:, :, 1]), 1)
    sums = quarter_total[:, 0].reshape(2, 2, HEADS, 2, HEAD)
    qv_grad = jnp.stack((sums[:, 1, :, 0].reshape(640), sums[:, 0, :, 1].reshape(640)))
    return (
        out_block[None, None],
        grad_block[None, None],
        home_total[None, 0:2],
        home_total[None, 2:4],
        qkv_grad.reshape(1, OWN, 3, 640),
        qv_grad[None],
        others[:, :, 1].reshape(OWN, 640).T[None],
        home_total[None, 4:6],
        shares[:, :, UP:DOWN].reshape(1, OWN, 2 * D),
        quarter_total[:, 1].reshape(1, 2 * D),
        shares[:, :, DOWN:].reshape(OWN, 2 * D).T[None],
    )


def solution(mesh):
    weights = P("section", ("ctx", "dp"), None, "tp")
    up = P("section", ("ctx", "dp"), "tp")
    down = P("section", "tp", ("ctx", "dp"))
    vector = P("section", None, None)
    return jax.shard_map(
        per_device,
        mesh=mesh,
        in_specs=(
            P("dp", None, "ctx", None),
            vector,
            vector,
            weights,
            P("section", None, "tp"),
            down,
            vector,
            up,
            P("section", "tp"),
            down,
            P("dp", None, "ctx", None),
        ),
        out_specs=(
            P("dp", "section", "ctx", None),
            P("dp", "section", "ctx", None),
            vector,
            vector,
            weights,
            P("section", None, "tp"),
            down,
            vector,
            up,
            P("section", "tp"),
            down,
        ),
        check_vma=False,
    )
```

```python
import functools

import jax
import jax.numpy as jnp
from jax import lax
from jax.experimental import pallas as pl
from jax.experimental.pallas import tpu as pltpu
from jax.sharding import PartitionSpec as P

MESH = pl.DeviceIdType.MESH
F32 = jnp.float32
BF16 = jnp.bfloat16
D = 1280
HEAD = 64
HEADS = 5
ROWS = 32
UNITS = ((0, 0), (1, 0), (0, 1), (1, 1))
KV, QO, UP, DOWN, COLS = (0, 640, 1280, 2560, 3840)
OWN = 40
CHIP = 80
GATHERED = (((0, 640, 384), (640, 640, 384)), ((1280, 640, 384), (1920, 1920, 1024)))
SCATTERED = (((0, 640, 384), (640, 640, 384)), ((1280, 1280, 640), (2560, 1280, 640)))
FIRST_FORWARD = "0ABCD1ABCDA2B3AC4BD5ACB6DAC7BDCDABACBADCBDCD"
LAST_PASSES = ("ABAABCADBCDBCABCADBCDBCADBCDBACDBCDACDAC", "aDAcaBDbcadcbadcabcbdabdabcdabdabcdcbdcd")
FIRST_BACKWARD = "AABACBADBCABDCAD0BCABD1CBDACBDCDACBD2ABCD3ACBDCD"
EPS = 1e-05
NEG = -1e30
MIB = 2**20


class Place:
    def __init__(self):
        self.s = lax.axis_index("section")
        self.z = lax.axis_index("ctx")
        self.dp = lax.axis_index("dp")
        self.t = lax.axis_index("tp")
        self.x = self.dp // 2
        self.c = self.dp % 2
        self.r = (self.s + self.t) % 2

    def core(self):
        return (self.s, self.z, self.x * 2 + 1 - self.c, self.t)

    def pair(self):
        return (self.s, self.z, self.dp, 1 - self.t)

    def other(self):
        return (1 - self.s, self.z, self.dp, 1 - self.t)

    def away(self, dz, dx):
        return (self.s, (self.z + dz + 4) % 4, (self.x + dx + 4) % 4 * 2 + self.c, self.t)

    def at(self, s, seq, t):
        return (s, self.z, self.x * 2 + seq, t)


def send(source, target, sems, device):
    copy = pltpu.make_async_remote_copy(
        src_ref=source,
        dst_ref=target,
        send_sem=sems[0],
        recv_sem=sems[1],
        device_id=device,
        device_id_type=MESH,
    )
    copy.start()
    return copy


def greet(devices):
    barrier = pltpu.get_barrier_semaphore()
    for device in devices:
        pl.semaphore_signal(barrier, inc=1, device_id=device, device_id_type=MESH)
    return barrier


def in_order(order, stages):
    for name in order:
        next(stages[name], None)
    for stage in stages.values():
        assert next(stage, "end") == "end"


def mm(a, b):
    return lax.dot_general(a, b, (((1,), (0,)), ((), ())), preferred_element_type=F32)


def mm_nt(a, b):
    return lax.dot_general(a, b, (((1,), (1,)), ((), ())), preferred_element_type=F32)


def mm_tn(a, b):
    return lax.dot_general(a, b, (((0,), (0,)), ((), ())), preferred_element_type=F32)


def layers_kernel(
    tokens,
    out_grad,
    shard,
    ln_gain,
    ln_bias,
    biases,
    branch_bias,
    up_share,
    down_share,
    other_share,
    home_total,
    quarter_total,
    out_block,
    grad_block,
    w,
    x_in,
    g_in,
    out_rows,
    grad_rows,
    a_all,
    c_all,
    g_all,
    ga_all,
    q_pad,
    kv_all,
    probs_one,
    probs_two,
    o_all,
    slopes,
    hidden,
    du_all,
    go_pad,
    dqkv,
    dkv_part,
    dkv_in,
    part,
    core_in,
    pair_out,
    pair_in,
    normed,
    recips,
    shares,
    grads,
    passing_q,
    passing_u,
    sums_q,
    sums_u,
    reduced,
    home_sum,
    quarter_sum,
    small,
    small_in,
    sems_s,
    sems_r,
    hop_sems,
    early_sems,
    gather_send,
    gather_recv,
    scatter_send,
    scatter_recv,
    core_sems,
    small_send,
    small_recv,
    rows_send,
    rows_recv,
    credit,
):
    me = Place()
    diagonal = (me.s, me.z, me.x * 2 + 1 - me.c, 1 - me.t)
    around = [me.away(1, 0), me.away(-1, 0), me.away(0, 1), me.away(0, -1)]
    devices = [me.core(), me.pair(), me.other(), me.away(2, 0), me.away(0, 2), diagonal] + around
    barrier = greet(devices)
    kinds = ((1, out_rows, out_block), (0, grad_rows, grad_block))
    quarters = tuple((r, c) for r in (0, 1) for c in (0, 1))
    for origin, _, _ in kinds:
        for r, c in quarters:
            itself = (me.s == origin) & (me.c == c) & (me.r == r)
            device = me.at(origin, c, (r + origin) % 2)

            @pl.when(jnp.logical_not(itself))
            def _():
                pl.semaphore_signal(barrier, inc=1, device_id=device, device_id_type=MESH)

    pl.semaphore_wait(barrier, 10 + 7)


    def gather_copy(chunk, half, group, kind):
        first, width, cut = GATHERED[chunk][half]
        parts = (cut, width - cut)
        i = (0, 0, -1, 1, 2)[group]
        by = (1, -1)[kind % 2]
        hop_from = (0, 0, -1, 1)[kind]
        part = (None, None, 0, 1)[kind]
        i, j = (hop_from, 0) if group == 0 else (i, hop_from)
        dz, dx = (j, i) if half == 0 else (i, j)
        top = ((me.z + dz + 4) % 4 * 4 + (me.x + dx + 4) % 4) * CHIP
        left = first + (cut if part == 1 else 0)
        columns = width if part is None else parts[part]
        ref = w.at[pl.ds(pl.multiple_of(top, 16), CHIP), pl.ds(left, columns)]
        along = (0, by) if (half == 0) == (group == 0) else (by, 0)
        return pltpu.make_async_remote_copy(
            src_ref=ref,
            dst_ref=ref,
            send_sem=gather_send.at[chunk, half, group, kind],
            recv_sem=gather_recv.at[chunk, half, group, kind],
            device_id=me.away(*along),
            device_id_type=MESH,
        )

    def gather_steps(chunk, half):
        def go(group, *kinds):
            for kind in kinds:
                gather_copy(chunk, half, group, kind).start()

        def landed(group, *kinds):
            for kind in kinds:
                gather_copy(chunk, half, group, kind).wait_recv()

        def first_axis():
            landed(0, 0)
            go(0, 2)
            go(2, 0, 1)
            landed(0, 1)
            go(0, 3)
            go(3, 0, 1)

        def turn(group):
            def run():
                landed(group, 0)
                go(group, 2)
                landed(group, 1)
                go(group, 3)

            return run

        def far():
            landed(0, 2, 3)
            go(4, 0, 1)

        def end():
            for group in (1, 2, 3, 4):
                landed(group, 2, 3)
            for group in range(5):
                for kind in range(4):
                    gather_copy(chunk, half, group, kind).wait_send()

        own = [lambda: go(0, 0, 1), lambda: go(1, 0, 1)]
        return own + [first_axis, turn(1), far, turn(2), turn(3), turn(4), end]


    def landing(chunk, half, group, slot):
        index = group * 3 + slot
        return index * CHIP, SCATTERED[chunk][half][0]

    def span(chunk, half, part):
        _, width, cut = SCATTERED[chunk][half]
        return ((0, cut), (cut, width - cut))[part]

    def sums_of(chunk):
        return (sums_q, sums_u)[chunk]

    def piece(chunk, half, group, j, part):
        left, columns = span(chunk, half, part)
        if group == 4:
            return sums_of(chunk).at[half, j % 4, :, pl.ds(left, columns)]
        dz, dx = (j, group) if half == 0 else (group, j)
        top = ((me.z + dz + 4) % 4 * 4 + (me.x + dx + 4) % 4) * CHIP
        place = pl.ds(SCATTERED[chunk][half][0] + left, columns)
        return grads.at[pl.ds(pl.multiple_of(top, 16), CHIP), place]

    def scatter_copy(chunk, half, group, kind):
        part = (0, 1, 1, 0, 0, 1)[kind]
        slot = (0, 0, 1, 2, 1, 2)[kind]
        by = (1, -1)[kind % 2]
        left, columns = span(chunk, half, part)
        if kind < 4:
            source = piece(chunk, half, group, (2, 2, 1, -1)[kind], part)
        else:
            passing = (passing_q, passing_u)[chunk]
            source = passing.at[half, group, :, pl.ds(left, columns)]
        row, column = landing(chunk, half, group, slot)
        along = (by, 0) if (half == 0) == (group != 4) else (0, by)
        return pltpu.make_async_remote_copy(
            src_ref=source,
            dst_ref=w.at[pl.ds(row, CHIP), pl.ds(column + left, columns)],
            send_sem=scatter_send.at[chunk, half, group, kind],
            recv_sem=scatter_recv.at[chunk, half, group, kind],
            device_id=me.away(*along),
            device_id_type=MESH,
        )

    def landed_part(chunk, half, group, slot, part):
        left, columns = span(chunk, half, part)
        row, column = landing(chunk, half, group, slot)
        return w[row : row + CHIP, column + left : column + left + columns].astype(F32)

    def scatter_begin(chunk, half, groups):
        for group in groups:
            for kind in range(4):
                scatter_copy(chunk, half, group, kind).start()

    def pass_on(chunk, half, group):
        for kind, part, j in ((0, 0, 1), (1, 1, -1)):
            left, columns = span(chunk, half, part)
            scatter_copy(chunk, half, group, kind).wait_recv()
            own = piece(chunk, half, group, j, part)[...].astype(F32)
            total = own + landed_part(chunk, half, group, 0, part)
            passing = (passing_q, passing_u)[chunk]
            passing[half, group, :, left : left + columns] = total.astype(BF16)
            scatter_copy(chunk, half, group, 4 + kind).start()

    def finish(chunk, half, group):
        for kind in (2, 3, 4, 5):
            scatter_copy(chunk, half, group, kind).wait_recv()
        for part in (0, 1):
            left, columns = span(chunk, half, part)
            total = (
                piece(chunk, half, group, 0, part)[...].astype(F32)
                + landed_part(chunk, half, group, 1, part)
                + landed_part(chunk, half, group, 2, part)
            )
            if group == 4:
                left = SCATTERED[chunk][half][0] + left
                reduced[:, left : left + columns] = total
            else:
                sums_of(chunk)[half, group, :, left : left + columns] = total.astype(BF16)

    def scatter_sent(chunk):
        for half in (0, 1):
            for group in range(5):
                for kind in range(6):
                    scatter_copy(chunk, half, group, kind).wait_send()

    def give_credit(chunk):
        for device in around:
            pl.semaphore_signal(credit.at[chunk], inc=1, device_id=device, device_id_type=MESH)

    def share_copies(chunk):
        theirs = pl.ds(pl.multiple_of((1 - me.c) * OWN, 8), OWN)
        place = pl.ds(pl.multiple_of(me.c * D, 128), D)
        targets = ((other_share, 0),) if chunk == 0 else ((up_share, UP), (down_share, DOWN))
        return [
            pltpu.make_async_remote_copy(
                src_ref=reduced.at[theirs, pl.ds(left, D)],
                dst_ref=target.at[:, place],
                send_sem=core_sems.at[left // D, 0],
                recv_sem=core_sems.at[left // D, 1],
                device_id=me.core(),
                device_id_type=MESH,
            )
            for target, left in targets
        ]

    def share(chunk):
        mine = pl.ds(pl.multiple_of(me.c * OWN, 8), OWN)
        place = pl.ds(pl.multiple_of(me.c * D, 128), D)
        for copy in share_copies(chunk):
            copy.start()
        targets = ((other_share, 0),) if chunk == 0 else ((up_share, UP), (down_share, DOWN))
        for target, left in targets:
            target[:, place] = reduced[mine, left : left + D]

    def scatter_steps(chunk, half):
        def onward(*groups):
            def run():
                for group in groups:
                    pass_on(chunk, half, group)

            return run

        def ending(*groups):
            def run():
                for group in groups:
                    finish(chunk, half, group)
                if len(groups) > 1:
                    scatter_begin(chunk, half, (4,))

            return run

        return [onward(2, 1), onward(3, 0), ending(2, 1, 3), ending(0), onward(4), ending(4)]


    def rows_copies(kind, act):
        origin, source, target = kinds[kind]

        @pl.when(me.s == origin)
        def _():
            place = target.at[pl.ds(pl.multiple_of(me.r * 64 + me.c * ROWS, ROWS), ROWS)]
            for seq, part in UNITS:
                for t in (0, 1):
                    itself = (me.s == part) & (me.c == seq) & (me.t == t)

                    @pl.when(jnp.logical_not(itself))
                    def _():
                        copy = pltpu.make_async_remote_copy(
                            src_ref=source.at[seq, part],
                            dst_ref=place,
                            send_sem=rows_send.at[kind, seq, part, t],
                            recv_sem=rows_recv.at[kind, me.r, me.c],
                            device_id=me.at(part, seq, t),
                            device_id_type=MESH,
                        )
                        if act == "start":
                            copy.start()
                        else:
                            copy.wait_send()

                    if act == "start":

                        @pl.when(itself)
                        def _():
                            place[...] = source[seq, part]

    def rows_arrive(kind):
        origin, source, target = kinds[kind]
        for r, c in quarters:
            itself = (me.s == origin) & (me.c == c) & (me.r == r)

            @pl.when(jnp.logical_not(itself))
            def _():
                pltpu.make_async_remote_copy(
                    src_ref=source.at[0, 0],
                    dst_ref=target.at[pl.ds(r * 64 + c * ROWS, ROWS)],
                    send_sem=rows_send.at[kind, 0, 0, 0],
                    recv_sem=rows_recv.at[kind, r, c],
                    device_id=me.core(),
                    device_id_type=MESH,
                ).wait_recv()


    def small_copies(step):
        rows = (8, 16, 16)[step]
        devices = (
            [me.core(), me.pair(), diagonal],
            [me.away(0, dx) for dx in (1, 2, 3)],
            [me.away(dz, 0) for dz in (1, 2, 3)],
        )[step]
        source = small.at[step, pl.ds(0, rows)]
        return [
            pltpu.make_async_remote_copy(
                src_ref=source,
                dst_ref=small_in.at[step, index, pl.ds(0, rows)],
                send_sem=small_send.at[step, index],
                recv_sem=small_recv.at[step, index],
                device_id=device,
                device_id_type=MESH,
            )
            for index, device in enumerate(devices)
        ]

    def vector_copy():
        return pltpu.make_async_remote_copy(
            src_ref=small.at[3, pl.ds(8, 8)],
            dst_ref=quarter_total.at[me.c],
            send_sem=core_sems.at[3, 0],
            recv_sem=core_sems.at[3, 1],
            device_id=me.core(),
            device_id_type=MESH,
        )

    def small_steps():
        small[0, 0:8, :] = home_sum[...]
        small[0, 8:16, :] = quarter_sum[...]
        for step in range(3):
            copies = small_copies(step)
            for copy in copies:
                copy.start()
            yield
            for copy in copies:
                copy.wait_recv()
            rows = (8, 16, 16)[step]
            total = small[step, 0:rows, :]
            for index in range(3):
                total = total + small_in[step, index, 0:rows, :]
            small[step + 1, 0:rows, :] = total
            if rows == 8:
                small[step + 1, 8:16, :] = small[step, 8:16, :]
        home_total[...] = small[3, 0:8, :]
        quarter_total[me.c] = small[3, 8:16, :]
        vector_copy().start()
        yield
        vector_copy().wait()
        for step in range(3):
            for copy in small_copies(step):
                copy.wait_send()

    counter = {}

    def new_sems(unit):
        index = counter.get(unit, 0)
        counter[unit] = index + 1
        return (sems_s.at[*unit, index], sems_r.at[*unit, index])

    flying = []

    def fly(source, target, unit, device):
        copy = send(source, target, new_sems(unit), device)
        flying.append(copy)
        return copy

    low_lanes = lax.broadcasted_iota(jnp.int32, (128, 640), 1) % 128 < HEAD
    low_half = lax.broadcasted_iota(jnp.int32, (128, 128), 1) < HEAD

    def first_rows(section, whole, rows_in):
        @pl.when(me.s == section)
        def _():
            mine = pl.ds(pl.multiple_of(me.r * 64 + me.c * ROWS, ROWS), ROWS)
            theirs = pl.ds(pl.multiple_of(me.r * 64 + (1 - me.c) * ROWS, ROWS), ROWS)
            for part in (0, 1):
                sems = (hop_sems.at[0, section, me.c, part], hop_sems.at[1, section, me.c, part])
                copy = send(whole.at[part, theirs], rows_in.at[me.c, part], sems, me.core())
                rows_in[me.c, part] = whole[part, mine, :]
                copy.wait_send()

    def rows_ready(section, rows_in, unit):
        @pl.when(jnp.logical_not((me.s == section) & (me.c == unit[0])))
        def _():
            pltpu.make_async_remote_copy(
                src_ref=rows_in.at[unit],
                dst_ref=rows_in.at[unit],
                send_sem=hop_sems.at[0, section, *unit],
                recv_sem=hop_sems.at[1, section, *unit],
                device_id=me.core(),
                device_id_type=MESH,
            ).wait_recv()

    def hop_copy(section, rows_out, rows_in, unit):
        return pltpu.make_async_remote_copy(
            src_ref=rows_out.at[unit],
            dst_ref=rows_in.at[unit],
            send_sem=hop_sems.at[2, section, *unit],
            recv_sem=hop_sems.at[1, section, *unit],
            device_id=me.other(),
            device_id_type=MESH,
        )

    def spread(rows, unit):
        own = rows.at[*unit, me.r, me.c]
        pair = fly(own, own, unit, me.pair())
        core = fly(own, own, unit, me.core())
        yield
        pair.wait_recv()
        arrived = rows.at[*unit, 1 - me.r, me.c]
        further = fly(arrived, arrived, unit, me.core())
        yield
        core.wait_recv()
        further.wait_recv()

    parts_flying = {}

    def before_part(unit):
        for copy in parts_flying.pop(unit, []):
            copy.wait_send()

    pair_flying = {}

    def collect(which, unit):
        slot = which % 2
        arriving = core_in.at[*unit, slot]
        core = send(part.at[*unit, :, 1 - me.c], arriving, new_sems(unit), me.core())
        parts_flying.setdefault(unit, []).append(core)
        yield
        core.wait_recv()
        theirs = part[*unit, 1 - me.r, me.c].astype(F32) + core_in[*unit, slot, 1 - me.r].astype(F32)
        if (unit, slot) in pair_flying:
            pair_flying[unit, slot].wait_send()
        pair_out[*unit, slot] = theirs.astype(BF16)
        pair = send(pair_out.at[*unit, slot], pair_in.at[*unit, slot], new_sems(unit), me.pair())
        pair_flying[unit, slot] = pair
        mine = part[*unit, me.r, me.c].astype(F32) + core_in[*unit, slot, me.r].astype(F32)
        yield
        pair.wait_recv()
        return mine + pair_in[*unit, slot].astype(F32)

    def norm(rows, which, unit, target):
        centred = rows - jnp.mean(rows, -1, keepdims=True)
        recip = lax.rsqrt(jnp.mean(centred * centred, -1, keepdims=True) + EPS)
        units = centred * recip
        normed[*unit, which] = units
        recips[*unit, which] = recip
        out = units * ln_gain[which : which + 1, :] + ln_bias[which : which + 1, :]
        target[*unit, me.r, me.c] = out.astype(BF16)

    def norm_back(grad, which, unit):
        units = normed[*unit, which]
        scaled = grad * ln_gain[which : which + 1, :]
        inner = (
            scaled
            - jnp.mean(scaled, -1, keepdims=True)
            - units * jnp.mean(scaled * units, -1, keepdims=True)
        )
        home_sum[which : which + 1, :] += jnp.sum(grad * units, 0, keepdims=True)
        home_sum[2 + which : 3 + which, :] += jnp.sum(grad, 0, keepdims=True)
        return inner * recips[*unit, which]

    def tiled(count, body):
        for n in range(count):
            body(n * 256)

    def back_through(rows, left, width, unit):
        def tile(n):
            out = mm_nt(rows, w[pl.ds(n, 256), left : left + width])
            part[*unit, :, :, :, pl.ds(n, 256)] = out.reshape(2, 2, ROWS, 256).astype(BF16)

        tiled(5, tile)

    def causal():
        query = me.z * 128 + lax.broadcasted_iota(jnp.int32, (128, 512), 0)
        key = lax.broadcasted_iota(jnp.int32, (128, 512), 1)
        return key <= query

    def keys_of(unit, head):
        if unit[1] == 0:
            return kv_all[unit[0], head, 0].reshape(512, 128)
        return kv_all[unit[0], head].reshape(1024, 128)


    def first_copy(backwards, unit, index):
        rows = (a_all, g_all)[backwards]
        ref = rows.at[*unit, 1 - me.r if index == 2 else me.r, me.c]
        return pltpu.make_async_remote_copy(
            src_ref=ref,
            dst_ref=ref,
            send_sem=early_sems.at[0, backwards, *unit, index],
            recv_sem=early_sems.at[1, backwards, *unit, index],
            device_id=me.pair() if index == 0 else me.core(),
            device_id_type=MESH,
        )

    def first_start(backwards, unit):
        if backwards:
            rows_ready(1, g_in, unit)
            g_all[*unit, me.r, me.c] = g_in[unit]
        else:
            rows_ready(0, x_in, unit)
            norm(x_in[unit].astype(F32), 0, unit, a_all)
        first_copy(backwards, unit, 0).start()
        first_copy(backwards, unit, 1).start()

    def first_more(backwards, unit):
        first_copy(backwards, unit, 0).wait_recv()
        first_copy(backwards, unit, 2).start()

    def first_end(backwards, unit):
        first_copy(backwards, unit, 1).wait_recv()
        first_copy(backwards, unit, 2).wait_recv()

    def first_spread(backwards, unit):
        first_start(backwards, unit)
        yield
        first_more(backwards, unit)
        yield
        first_end(backwards, unit)

    up, down = (me.away(1, 0), me.away(-1, 0))
    first, second = (pl.ds(0, 64), pl.ds(64, 64))

    def forward(unit, section):
        seq, micro = unit
        probs = (probs_one, probs_two)[micro]
        if section == 1:
            yield from first_spread(0, unit)
        rows = x_in[unit].astype(F32)
        a = a_all[unit].reshape(128, D)
        pairs = (mm(a, w[:, KV:QO]) + biases[me.c, 0:1, KV:QO]).astype(BF16)
        for head in range(HEADS):
            kv_all[seq, head, micro, me.z] = pairs[:, head * 128 : head * 128 + 128]

        def block(place, half):
            return kv_all.at[seq, :, micro, (me.z + place) % 4, half]

        up_first = fly(block(0, first), block(0, first), unit, up)
        down_second = fly(block(0, second), block(0, second), unit, down)
        up_second = fly(block(0, second), block(0, second), unit, up)
        down_first = fly(block(0, first), block(0, first), unit, down)
        queries = jnp.where(low_lanes, mm(a, w[:, QO:UP]) + biases[me.c, 0:1, QO:UP], 0.0)
        queries = (queries.astype(BF16).astype(F32) * HEAD**-0.5).astype(BF16)
        for head in range(HEADS):
            q_pad[*unit, head] = queries[:, head * 128 : head * 128 + 128]
        yield
        up_first.wait_recv()
        far_up = fly(block(3, first), block(3, first), unit, up)
        down_second.wait_recv()
        far_down = fly(block(1, second), block(1, second), unit, down)
        yield
        for copy in (up_second, down_first, far_up, far_down):
            copy.wait_recv()

        def one_head(head):
            pairs = keys_of(unit, head)
            scores = mm_nt(q_pad[*unit, head], pairs)
            recent = jnp.where(causal(), scores[:, -512:], NEG)
            scores = recent if micro == 0 else jnp.concatenate((scores[:, :512], recent), 1)
            weights = jnp.exp(scores - jnp.max(scores, -1, keepdims=True))
            share = 1.0 / jnp.sum(weights, -1, keepdims=True)
            shares[*unit, head] = share
            weights = weights.astype(BF16)
            probs[seq, head] = weights
            out = jnp.where(low_half, 0.0, mm(weights, pairs) * share)
            o_all[*unit, :, head * 128 : head * 128 + 128] = out.astype(BF16)

        for head in range(HEADS):
            one_head(head)
        back_through(o_all[unit], QO, 640, unit)
        total = yield from collect(0, unit)
        rows = rows + total + branch_bias[0:1, :]
        norm(rows, 1, unit, c_all)
        yield from spread(c_all, unit)

        def up_tile(n):
            columns = pl.ds(n, 256)
            pre = mm(c_all[unit].reshape(128, D), w[:, pl.ds(UP + n, 256)]) + biases[me.c, 1:2, columns]
            scale = 0.7978845608028654
            square = pre * pre
            curve = jnp.tanh(scale * (pre + 0.044715 * (square * pre)))
            half = 0.5 * (1.0 + curve)
            hidden[*unit, :, columns] = (pre * half).astype(BF16)
            slope = half + 0.5 * pre * (1.0 - curve * curve) * (scale * (1.0 + 3 * 0.044715 * square))
            slopes[*unit, :, columns] = slope.astype(BF16)

        tiled(5, up_tile)
        before_part(unit)
        back_through(hidden[unit], DOWN, 1280, unit)
        total = yield from collect(1, unit)
        rows = rows + total + branch_bias[1:2, :]
        out_rows[unit] = rows.astype(BF16)
        if section == 0:
            hop_copy(0, out_rows, x_in, unit).start()

    def backward(unit, section):
        seq, micro = unit
        probs = (probs_one, probs_two)[micro]
        if section == 0:
            yield from first_spread(1, unit)
        rows = g_in[unit].astype(F32)
        home_sum[5:6, :] += jnp.sum(rows, 0, keepdims=True)

        def down_tile(n):
            columns = pl.ds(n, 256)
            grad = mm(g_all[unit].reshape(128, D), w[:, pl.ds(DOWN + n, 256)])
            grad = (grad * slopes[*unit, :, columns].astype(F32)).astype(BF16)
            du_all[*unit, :, columns] = grad
            quarter_sum[1:2, columns] += jnp.sum(grad.astype(F32), 0, keepdims=True)

        tiled(5, down_tile)
        before_part(unit)
        back_through(du_all[unit], UP, 1280, unit)
        total = yield from collect(2, unit)
        rows = rows + norm_back(total, 1, unit)
        low = rows.astype(BF16)
        ga_all[*unit, me.r, me.c] = low
        home_sum[4:5, :] += jnp.sum(low.astype(F32), 0, keepdims=True)
        yield from spread(ga_all, unit)
        grad = mm(ga_all[unit].reshape(128, D), w[:, QO:UP])
        go_pad[unit] = jnp.where(low_lanes, 0.0, grad).astype(BF16)

        def one_head(head):
            pairs = keys_of(unit, head)
            columns = pl.ds(head * 128, 128)
            out_grads = (go_pad[*unit, :, columns].astype(F32) * shares[*unit, head]).astype(BF16)
            queries = q_pad[*unit, head]
            low = probs[seq, head]
            pulled = low.astype(F32) * mm_nt(out_grads, pairs)
            delta = shares[*unit, head] * jnp.sum(pulled, -1, keepdims=True)
            grad = (pulled - low.astype(F32) * delta).astype(BF16)
            query_grad = mm(grad, pairs) * HEAD**-0.5
            place = pl.ds(QO + head * 128, 128)
            dqkv[*unit, :, place] = jnp.where(low_half, query_grad, 0.0).astype(BF16)
            pairs_grad = mm_tn(grad, queries) + mm_tn(low, out_grads)
            if micro == 1:
                pairs_grad = pairs_grad.reshape(2, 4, 128, 128)
                dkv_part[seq, head, 0] = pairs_grad[0].astype(BF16)
                dkv_part[seq, head, 1] = pairs_grad[1].astype(BF16)
            else:
                total = dkv_part[seq, head, 0].astype(F32) + pairs_grad.reshape(4, 128, 128)
                dkv_part[seq, head, 0] = total.astype(BF16)

        for head in range(HEADS):
            one_head(head)
        far, right, left = ((me.z + 2) % 4, (me.z + 1) % 4, (me.z + 3) % 4)

        def block(place, half):
            return dkv_part.at[seq, :, micro, place, half]

        def land(slot, half):
            return dkv_in.at[*unit, slot, :, half]

        far_up = fly(block(far, first), land(0, first), unit, up)
        far_down = fly(block(far, second), land(0, second), unit, down)
        up_own = fly(block(right, second), land(1, second), unit, up)
        down_own = fly(block(left, first), land(2, first), unit, down)
        yield
        far_up.wait_recv()
        total = dkv_part[seq, :, micro, right, 0:64].astype(F32) + dkv_in[*unit, 0, :, 0:64].astype(F32)
        dkv_in[*unit, 0, :, 0:64] = total.astype(BF16)
        up_sum = fly(land(0, first), land(1, first), unit, up)
        far_down.wait_recv()
        total = dkv_part[seq, :, micro, left, 64:128].astype(F32) + dkv_in[*unit, 0, :, 64:128].astype(F32)
        dkv_in[*unit, 0, :, 64:128] = total.astype(BF16)
        down_sum = fly(land(0, second), land(2, second), unit, down)
        yield
        for copy in (up_own, down_own, up_sum, down_sum):
            copy.wait_recv()
        for head in range(HEADS):
            total = dkv_part[seq, head, micro, me.z].astype(F32)
            for slot in (1, 2):
                total = total + dkv_in[*unit, slot, head].astype(F32)
            dqkv[*unit, :, head * 128 : head * 128 + 128] = total.astype(BF16)
        before_part(unit)
        back_through(dqkv[unit], KV, 1280, unit)
        total = yield from collect(3, unit)
        rows = rows + norm_back(total, 0, unit)
        grad_rows[unit] = rows.astype(BF16)
        if section == 1:
            hop_copy(1, grad_rows, g_in, unit).start()

    def grad_wide(rows, other, left):
        def tile(n):
            out = mm_tn(rows[...].reshape(512, D), other[:, :, :, pl.ds(n, 256)].reshape(512, 256))
            grads[:, pl.ds(left + n, 256)] = out.astype(BF16)

        tiled(5, tile)

    def grad_narrow(rows, other, begin, left, more):
        def tile(n):
            place = pl.ds(n, 256)
            turned = rows[:, :, :, :, :, place].reshape(512, 256)
            out = mm_tn(turned, other[:, :, :, begin : begin + 640].reshape(512, 640))
            if more:
                out = out + grads[place, left : left + 640].astype(F32)
            grads[place, left : left + 640] = out.astype(BF16)

        tiled(5, tile)

    home_sum[...] = jnp.zeros_like(home_sum)
    quarter_sum[...] = jnp.zeros_like(quarter_sum)
    swap = send(shard.at[1 - me.c], reduced.at[pl.ds(0, OWN)], (core_sems.at[4, 0], core_sems.at[4, 1]), me.core())
    first_rows(0, tokens, x_in)
    first_rows(1, out_grad, g_in)
    swap.wait()
    row = pl.multiple_of((me.z * 4 + me.x) * CHIP, 16)
    for start in range(0, COLS, 640):
        columns = slice(start, start + 640)
        mine = shard[me.c, :, columns]
        theirs = reduced[0:OWN, columns]
        lower = jnp.where(me.c == 0, mine, theirs)
        upper = jnp.where(me.c == 0, theirs, mine)
        w[pl.ds(row, CHIP), columns] = jnp.concatenate((lower, upper), 0).astype(BF16)

    def each(steps):
        for step in steps:
            step()
            yield

    def landed_all():
        for copy in flying + list(pair_flying.values()):
            copy.wait_send()
        for unit in UNITS:
            before_part(unit)
        flying.clear()
        pair_flying.clear()

    def begin(backwards):
        lower, upper = (gather_steps(0, 0), gather_steps(0, 1))
        heavy_z, heavy_x = (gather_steps(1, 0), gather_steps(1, 1))

        def both(*indices):
            for index in indices:
                lower[index]()
                upper[index]()

        both(0, 1)
        for unit in UNITS:
            first_start(backwards, unit)
        both(2, 3, 4)
        heavy_x[0]()
        heavy_z[0]()
        for unit in UNITS:
            first_more(backwards, unit)
        both(5, 6, 7, 8)
        for unit in UNITS:
            first_end(backwards, unit)
        return [
            heavy_x[1:3],
            heavy_x[3:5],
            heavy_z[1:3],
            heavy_x[5:7],
            heavy_z[3:5],
            heavy_x[7:8] + heavy_z[5:6],
            heavy_z[6:8],
            heavy_x[8:] + heavy_z[8:],
        ]

    def scatter_down():
        give_credit(1)
        grad_wide(g_all, hidden, DOWN)
        pl.semaphore_wait(credit.at[1], 4)
        scatter_begin(1, 1, (2, 1, 3, 0))

    def scatter_parts():
        lower, upper = (scatter_steps(1, 1), scatter_steps(1, 0))
        return [
            [scatter_down],
            [lambda: grad_wide(c_all, du_all, UP)],
            [lambda: scatter_begin(1, 0, (2, 1, 3, 0)), lambda: grad_narrow(ga_all, o_all, 0, QO, False)],
            lower[0:2],
            upper[0:2],
            lower[2:4],
            upper[2:4],
            lower[4:6],
            upper[4:6],
            [lambda: share(1)],
        ]

    def run(steps):
        for step in steps:
            step()


    def scatter_last(waiting):
        smalls = small_steps()
        give_credit(0)
        grad_narrow(a_all, dqkv, QO, QO, True)
        pl.semaphore_wait(credit.at[0], 4)
        scatter_begin(0, 1, (2, 1, 3, 0))
        for steps in waiting[:1]:
            run(steps)
        grad_narrow(a_all, dqkv, KV, KV, False)
        scatter_begin(0, 0, (2, 1, 3, 0))
        column_sum = jnp.sum(dqkv[...].astype(F32), axis=(0, 1, 2))
        quarter_sum[0:1, :] += column_sum.reshape(1, D)
        next(smalls, None)
        for steps in waiting[1:3]:
            run(steps)
        next(smalls, None)
        lower, upper = (scatter_steps(0, 1), scatter_steps(0, 0))
        for index, steps in enumerate((lower[0:2], upper[0:2])):
            run(steps)
            run(sum(waiting[3 + index : 4 + index], []))
            next(smalls, None)
        for index, steps in enumerate((lower[2:4], upper[2:4])):
            run(steps)
            run(sum(waiting[5 + index : 6 + index], []))
        next(smalls, None)
        run(lower[4:5] + upper[4:5])
        next(smalls, None)
        run(lower[5:] + upper[5:])
        next(smalls, None)
        share(0)

    @pl.when(me.s == 0)
    def _():
        stages = dict(zip("ABCD", [forward(unit, 0) for unit in UNITS]))
        steps = each([functools.partial(run, steps) for steps in begin(0)])
        stages.update(dict.fromkeys("01234567", steps))
        in_order(FIRST_FORWARD, stages)
        landed_all()
        for unit in UNITS:
            hop_copy(0, out_rows, x_in, unit).wait_send()

    @pl.when(me.s == 1)
    def _():
        for steps in begin(1):
            run(steps)
        counter.clear()
        stages = dict(zip("ABCD", [forward(unit, 1) for unit in UNITS]))
        stages.update(zip("abcd", [backward(unit, 1) for unit in UNITS[2:] + UNITS[:2]]))
        in_order("".join(LAST_PASSES), stages)
        landed_all()

    rows_copies(0, "start")

    @pl.when(me.s == 1)
    def _():
        for unit in UNITS:
            hop_copy(1, grad_rows, g_in, unit).wait_send()
        for steps in scatter_parts():
            run(steps)
        scatter_last([])

    @pl.when(me.s == 0)
    def _():
        for unit in UNITS:
            counter[unit] = 16
        stages = dict(zip("ABCD", [backward(unit, 0) for unit in UNITS[2:] + UNITS[:2]]))
        steps = scatter_parts()
        stages.update(dict.fromkeys("0123", each([functools.partial(run, part) for part in steps[:4]])))
        in_order(FIRST_BACKWARD, stages)
        landed_all()
        rows_copies(1, "start")
        scatter_last(steps[4:])

    rows_arrive(0)
    rows_arrive(1)
    for copy in share_copies(0) + share_copies(1):
        copy.wait()
    scatter_sent(0)
    scatter_sent(1)
    for unit in UNITS:
        for index in range(3):
            first_copy(0, unit, index).wait_send()
            first_copy(1, unit, index).wait_send()
    rows_copies(0, "wait")
    rows_copies(1, "wait")


def lower_of(block):
    return block[:, :HEAD]


def upper_of(block):
    return block[:, HEAD:]


def pack_kernel(w_qkv, w_out, w_up, w_down, qv_bias, up_bias, shard, biases):
    qkv = w_qkv[...].astype(F32)
    out_turned = w_out[...].astype(F32).T
    none = jnp.zeros((1, HEAD), F32)
    for head in range(2 * HEADS):
        quarter, place = (head // HEADS, head % HEADS * 128)
        columns = slice(head * HEAD, head * HEAD + HEAD)
        shard[quarter, :, KV + place : KV + place + 128] = jnp.concatenate(
            (qkv[:, 1, columns], qkv[:, 2, columns]), 1
        )
        shard[quarter, :, QO + place : QO + place + 128] = jnp.concatenate(
            (qkv[:, 0, columns], out_turned[:, columns]), 1
        )
        biases[quarter, 0:1, KV + place : KV + place + 128] = jnp.concatenate((none, qv_bias[1:2, columns]), 1)
        biases[quarter, 0:1, QO + place : QO + place + 128] = jnp.concatenate((qv_bias[0:1, columns], none), 1)
    for quarter in (0, 1):
        columns = slice(quarter * D, quarter * D + D)
        shard[quarter, :, UP:DOWN] = w_up[:, columns].astype(F32)
        shard[quarter, :, DOWN:COLS] = w_down[columns, :].astype(F32).T
        biases[quarter, 1:2, :] = up_bias[0:1, columns]


def unpack_kernel(
    other_share,
    down_share,
    home_total,
    quarter_total,
    qkv_grad,
    out_grad,
    down_grad,
    gain_grad,
    bias_grad,
    qv_grad,
    branch_grad,
    up_bias_grad,
):
    def blocks(rows, left):
        return [rows(head // HEADS, left + head % HEADS * 128) for head in range(2 * HEADS)]

    def of_share(quarter, column):
        return other_share[:, quarter * D + column : quarter * D + column + 128]

    def of_sums(quarter, column):
        return quarter_total[quarter, 0:1, column : column + 128]

    pairs, others = (blocks(of_share, KV), blocks(of_share, QO))
    for n in range(HEADS):
        columns = slice(n * 128, n * 128 + 128)
        two = slice(2 * n, 2 * n + 2)
        qkv_grad[:, 0, columns] = jnp.concatenate([lower_of(x) for x in others[two]], 1)
        qkv_grad[:, 1, columns] = jnp.concatenate([lower_of(x) for x in pairs[two]], 1)
        qkv_grad[:, 2, columns] = jnp.concatenate([upper_of(x) for x in pairs[two]], 1)
        out_grad[columns, :] = jnp.concatenate([upper_of(x) for x in others[two]], 1).T
    pairs, others = (blocks(of_sums, KV), blocks(of_sums, QO))
    for n in range(HEADS):
        columns = slice(n * 128, n * 128 + 128)
        two = slice(2 * n, 2 * n + 2)
        qv_grad[0:1, columns] = jnp.concatenate([lower_of(x) for x in others[two]], 1)
        qv_grad[1:2, columns] = jnp.concatenate([upper_of(x) for x in pairs[two]], 1)
    for n in range(0, 2 * D, 256):
        down_grad[n : n + 256, :] = down_share[:, n : n + 256].T
    gain_grad[...] = home_total[0:2, :]
    bias_grad[...] = home_total[2:4, :]
    branch_grad[...] = home_total[4:6, :]
    for quarter in (0, 1):
        up_bias_grad[0:1, quarter * D : quarter * D + D] = quarter_total[quarter, 1:2, :]


def vmem(shape, kind):
    return pltpu.VMEM(shape, kind)


def call(kernel, name, operands, outs, scratch=(), flops=0, **params):
    whole = pl.BlockSpec(memory_space=pltpu.VMEM)
    moved = sum(a.size * a.dtype.itemsize for a in operands)
    return pl.pallas_call(
        kernel,
        name=name,
        out_shape=[jax.ShapeDtypeStruct(shape, kind) for shape, kind in outs],
        in_specs=[whole] * len(operands),
        out_specs=[whole] * len(outs),
        scratch_shapes=scratch,
        cost_estimate=pl.CostEstimate(flops=flops, bytes_accessed=moved, transcendentals=0),
        compiler_params=pltpu.CompilerParams(**params),
    )(*operands)


def per_device(
    tokens, ln_gain, ln_bias, w_qkv, qv_bias, w_out, branch_bias, w_up, up_bias, w_down, out_grad
):
    dma = pltpu.SemaphoreType.DMA
    shard, biases = call(
        pack_kernel,
        "pack",
        [w_qkv[0], w_out[0], w_up[0], w_down[0], qv_bias[0], up_bias],
        [((2, OWN, COLS), F32), ((2, 2, D), F32)],
        vmem_limit_bytes=32 * MIB,
    )
    up_share, down_share, other_share, home_total, quarter_total, out_block, grad_block = call(
        layers_kernel,
        "layers",
        [
            tokens[0],
            out_grad[0],
            shard,
            ln_gain[0],
            ln_bias[0],
            biases,
            branch_bias[0],
        ],
        [
            ((OWN, 2 * D), F32),
            ((OWN, 2 * D), F32),
            ((OWN, 2 * D), F32),
            ((8, D), F32),
            ((2, 8, D), F32),
            ((128, D), BF16),
            ((128, D), BF16),
        ],
        [
            vmem((D, COLS), BF16),
            vmem((2, 2, ROWS, D), BF16),
            vmem((2, 2, ROWS, D), BF16),
            vmem((2, 2, ROWS, D), BF16),
            vmem((2, 2, ROWS, D), BF16),
            vmem((2, 2, 2, 2, ROWS, D), BF16),
            vmem((2, 2, 2, 2, ROWS, D), BF16),
            vmem((2, 2, 2, 2, ROWS, D), BF16),
            vmem((2, 2, 2, 2, ROWS, D), BF16),
            vmem((2, 2, HEADS, 128, 128), BF16),
            vmem((2, HEADS, 2, 4, 128, 128), BF16),
            vmem((2, HEADS, 128, 512), BF16),
            vmem((2, HEADS, 128, 1024), BF16),
            vmem((2, 2, 128, 640), BF16),
            vmem((2, 2, 128, D), BF16),
            vmem((2, 2, 128, D), BF16),
            vmem((2, 2, 128, D), BF16),
            vmem((2, 2, 128, 640), BF16),
            vmem((2, 2, 128, D), BF16),
            vmem((2, HEADS, 2, 4, 128, 128), BF16),
            vmem((2, 2, 3, HEADS, 128, 128), BF16),
            vmem((2, 2, 2, 2, ROWS, D), BF16),
            vmem((2, 2, 2, 2, ROWS, D), BF16),
            vmem((2, 2, 2, ROWS, D), BF16),
            vmem((2, 2, 2, ROWS, D), BF16),
            vmem((2, 2, 2, ROWS, D), F32),
            vmem((2, 2, 2, ROWS, 1), F32),
            vmem((2, 2, HEADS, 128, 1), F32),
            vmem((D, COLS), BF16),
            vmem((2, 5, CHIP, 640), BF16),
            vmem((2, 5, CHIP, 1280), BF16),
            vmem((2, 4, CHIP, 640), BF16),
            vmem((2, 4, CHIP, 1280), BF16),
            vmem((CHIP, COLS), F32),
            vmem((8, D), F32),
            vmem((8, D), F32),
            vmem((4, 16, D), F32),
            vmem((3, 3, 16, D), F32),
            dma((2, 2, 32)),
            dma((2, 2, 32)),
            dma((3, 2, 2, 2)),
            dma((2, 2, 2, 2, 3)),
            dma((2, 2, 5, 4)),
            dma((2, 2, 5, 4)),
            dma((2, 2, 5, 6)),
            dma((2, 2, 5, 6)),
            dma((5, 2)),
            dma((3, 3)),
            dma((3, 3)),
            dma((2, 2, 2, 2)),
            dma((2, 2, 2)),
            pltpu.SemaphoreType.REGULAR((2,)),
        ],
        2 * 512 * D * COLS * 3,
        collective_id=0,
        has_side_effects=True,
        vmem_limit_bytes=64 * MIB,
    )
    qkv_grad, w_out_grad, down_grad, gain_grad, bias_grad, qv_grad, branch_grad, up_bias_grad = call(
        unpack_kernel,
        "unpack",
        [other_share, down_share, home_total, quarter_total],
        [
            ((OWN, 3, 640), F32),
            ((640, OWN), F32),
            ((2 * D, OWN), F32),
            ((2, D), F32),
            ((2, D), F32),
            ((2, 640), F32),
            ((2, D), F32),
            ((1, 2 * D), F32),
        ],
        vmem_limit_bytes=32 * MIB,
    )
    return (
        out_block[None, None],
        grad_block[None, None],
        gain_grad[None],
        bias_grad[None],
        qkv_grad[None],
        qv_grad[None],
        w_out_grad[None],
        branch_grad[None],
        up_share[None],
        up_bias_grad,
        down_grad[None],
    )


def solution(mesh):
    weights = P("section", ("ctx", "dp"), None, "tp")
    up = P("section", ("ctx", "dp"), "tp")
    down = P("section", "tp", ("ctx", "dp"))
    vector = P("section", None, None)
    return jax.shard_map(
        per_device,
        mesh=mesh,
        in_specs=(
            P("dp", None, "ctx", None),
            vector,
            vector,
            weights,
            P("section", None, "tp"),
            down,
            vector,
            up,
            P("section", "tp"),
            down,
            P("dp", None, "ctx", None),
        ),
        out_specs=(
            P("dp", "section", "ctx", None),
            P("dp", "section", "ctx", None),
            vector,
            vector,
            weights,
            P("section", None, "tp"),
            down,
            vector,
            up,
            P("section", "tp"),
            down,
        ),
        check_vma=False,
    )
```

```python
import functools

import jax
import jax.numpy as jnp
from jax import lax
from jax.experimental import pallas as pl
from jax.experimental.pallas import tpu as pltpu
from jax.sharding import PartitionSpec as P

MESH = pl.DeviceIdType.MESH
F32 = jnp.float32
BF16 = jnp.bfloat16
D = 1280
HEAD = 64
HEADS = 5
ROWS = 32
UNITS = ((0, 0), (1, 0), (0, 1), (1, 1))
KV, QO, UP, DOWN, COLS = (0, 640, 1280, 2560, 3840)
OWN = 40
CHIP = 80
GATHERED = (((0, 640, 384), (640, 640, 384)), ((1280, 640, 384), (1920, 1920, 1024)))
SCATTERED = (((0, 512, 256), (512, 768, 384)), ((1280, 1024, 512), (2304, 1536, 768)))
FIRST_FORWARD = "0ABCD1ABCDA2B3AC4BD5ACB6DAC7BDCDABCDABCDABCD"
LAST_PASSES = ("ABAABCADBCDBCABCADBCDBCADBCDBACDBCDACDAC", "aDAcaBDbcadcbadcabcbdabdabcdabdabcdcbdcd")
FIRST_BACKWARD = "AABACBADBCABDCAD0BCABD1CBDACBDCDACBD2ABCD3ACBDCD"
EPS = 1e-05
NEG = -1e30
MIB = 2**20


class Place:
    def __init__(self):
        self.s = lax.axis_index("section")
        self.z = lax.axis_index("ctx")
        self.dp = lax.axis_index("dp")
        self.t = lax.axis_index("tp")
        self.x = self.dp // 2
        self.c = self.dp % 2
        self.r = (self.s + self.t) % 2

    def core(self):
        return (self.s, self.z, self.x * 2 + 1 - self.c, self.t)

    def pair(self):
        return (self.s, self.z, self.dp, 1 - self.t)

    def other(self):
        return (1 - self.s, self.z, self.dp, 1 - self.t)

    def away(self, dz, dx):
        return (self.s, (self.z + dz + 4) % 4, (self.x + dx + 4) % 4 * 2 + self.c, self.t)

    def at(self, s, seq, t):
        return (s, self.z, self.x * 2 + seq, t)


def send(source, target, sems, device):
    copy = pltpu.make_async_remote_copy(
        src_ref=source,
        dst_ref=target,
        send_sem=sems[0],
        recv_sem=sems[1],
        device_id=device,
        device_id_type=MESH,
    )
    copy.start()
    return copy


def greet(devices):
    barrier = pltpu.get_barrier_semaphore()
    for device in devices:
        pl.semaphore_signal(barrier, inc=1, device_id=device, device_id_type=MESH)
    return barrier


def in_order(order, stages):
    for name in order:
        next(stages[name], None)
    for stage in stages.values():
        assert next(stage, "end") == "end"


def mm(a, b):
    return lax.dot_general(a, b, (((1,), (0,)), ((), ())), preferred_element_type=F32)


def mm_nt(a, b):
    return lax.dot_general(a, b, (((1,), (1,)), ((), ())), preferred_element_type=F32)


def mm_tn(a, b):
    return lax.dot_general(a, b, (((0,), (0,)), ((), ())), preferred_element_type=F32)


def layers_kernel(
    tokens,
    out_grad,
    w_qkv,
    w_out,
    w_up,
    w_down,
    qv_bias,
    up_bias,
    ln_gain,
    ln_bias,
    branch_bias,
    up_share,
    down_share,
    other_share,
    home_total,
    quarter_total,
    out_block,
    grad_block,
    shard,
    biases,
    w,
    x_in,
    g_in,
    out_rows,
    grad_rows,
    a_all,
    c_all,
    g_all,
    ga_all,
    q_pad,
    kv_all,
    probs_one,
    probs_two,
    o_all,
    slopes,
    hidden,
    du_all,
    go_pad,
    dqkv,
    dkv_part,
    dkv_in,
    part,
    core_in,
    pair_out,
    pair_in,
    normed,
    recips,
    shares,
    grads,
    passing_q,
    passing_u,
    sums_q,
    sums_u,
    reduced,
    home_sum,
    quarter_sum,
    small,
    small_in,
    sems_s,
    sems_r,
    hop_sems,
    early_sems,
    gather_send,
    gather_recv,
    scatter_send,
    scatter_recv,
    core_sems,
    small_send,
    small_recv,
    rows_send,
    rows_recv,
    credit,
):
    me = Place()
    diagonal = (me.s, me.z, me.x * 2 + 1 - me.c, 1 - me.t)
    around = [me.away(1, 0), me.away(-1, 0), me.away(0, 1), me.away(0, -1)]
    devices = [me.core(), me.pair(), me.other(), me.away(2, 0), me.away(0, 2), diagonal] + around
    barrier = greet(devices)
    kinds = ((1, out_rows, out_block), (0, grad_rows, grad_block))
    quarters = tuple((r, c) for r in (0, 1) for c in (0, 1))
    for origin, _, _ in kinds:
        for r, c in quarters:
            itself = (me.s == origin) & (me.c == c) & (me.r == r)
            device = me.at(origin, c, (r + origin) % 2)

            @pl.when(jnp.logical_not(itself))
            def _():
                pl.semaphore_signal(barrier, inc=1, device_id=device, device_id_type=MESH)

    pl.semaphore_wait(barrier, 10 + 7)


    def gather_copy(chunk, half, group, kind):
        first, width, cut = GATHERED[chunk][half]
        parts = (cut, width - cut)
        i = (0, 0, -1, 1, 2)[group]
        by = (1, -1)[kind % 2]
        hop_from = (0, 0, -1, 1)[kind]
        part = (None, None, 0, 1)[kind]
        i, j = (hop_from, 0) if group == 0 else (i, hop_from)
        dz, dx = (j, i) if half == 0 else (i, j)
        top = ((me.z + dz + 4) % 4 * 4 + (me.x + dx + 4) % 4) * CHIP
        left = first + (cut if part == 1 else 0)
        columns = width if part is None else parts[part]
        ref = w.at[pl.ds(pl.multiple_of(top, 16), CHIP), pl.ds(left, columns)]
        along = (0, by) if (half == 0) == (group == 0) else (by, 0)
        return pltpu.make_async_remote_copy(
            src_ref=ref,
            dst_ref=ref,
            send_sem=gather_send.at[chunk, half, group, kind],
            recv_sem=gather_recv.at[chunk, half, group, kind],
            device_id=me.away(*along),
            device_id_type=MESH,
        )

    def gather_steps(chunk, half):
        def go(group, *kinds):
            for kind in kinds:
                gather_copy(chunk, half, group, kind).start()

        def landed(group, *kinds):
            for kind in kinds:
                gather_copy(chunk, half, group, kind).wait_recv()

        def first_axis():
            landed(0, 0)
            go(0, 2)
            go(2, 0, 1)
            landed(0, 1)
            go(0, 3)
            go(3, 0, 1)

        def turn(group):
            def run():
                landed(group, 0)
                go(group, 2)
                landed(group, 1)
                go(group, 3)

            return run

        def far():
            landed(0, 2, 3)
            go(4, 0, 1)

        def end():
            for group in (1, 2, 3, 4):
                landed(group, 2, 3)
            for group in range(5):
                for kind in range(4):
                    gather_copy(chunk, half, group, kind).wait_send()

        own = [lambda: go(0, 0, 1), lambda: go(1, 0, 1)]
        return own + [first_axis, turn(1), far, turn(2), turn(3), turn(4), end]


    def landing(chunk, half, group, slot):
        index = group * 3 + slot
        return index * CHIP, SCATTERED[chunk][half][0]

    def span(chunk, half, part):
        _, width, cut = SCATTERED[chunk][half]
        return ((0, cut), (cut, width - cut))[part]

    def offset(chunk, half):
        return SCATTERED[chunk][half][0] - SCATTERED[chunk][0][0]

    def sums_of(chunk):
        return (sums_q, sums_u)[chunk]

    def piece(chunk, half, group, j, part):
        left, columns = span(chunk, half, part)
        if group == 4:
            return sums_of(chunk).at[j % 4, :, pl.ds(offset(chunk, half) + left, columns)]
        dz, dx = (j, group) if half == 0 else (group, j)
        top = ((me.z + dz + 4) % 4 * 4 + (me.x + dx + 4) % 4) * CHIP
        place = pl.ds(SCATTERED[chunk][half][0] + left, columns)
        return grads.at[pl.ds(pl.multiple_of(top, 16), CHIP), place]

    def scatter_copy(chunk, half, group, kind):
        part = (0, 1, 1, 0, 0, 1)[kind]
        slot = (0, 0, 1, 2, 1, 2)[kind]
        by = (1, -1)[kind % 2]
        left, columns = span(chunk, half, part)
        if kind < 4:
            source = piece(chunk, half, group, (2, 2, 1, -1)[kind], part)
        else:
            passing = (passing_q, passing_u)[chunk]
            source = passing.at[group, :, pl.ds(offset(chunk, half) + left, columns)]
        row, column = landing(chunk, half, group, slot)
        along = (by, 0) if (half == 0) == (group != 4) else (0, by)
        return pltpu.make_async_remote_copy(
            src_ref=source,
            dst_ref=w.at[pl.ds(row, CHIP), pl.ds(column + left, columns)],
            send_sem=scatter_send.at[chunk, half, group, kind],
            recv_sem=scatter_recv.at[chunk, half, group, kind],
            device_id=me.away(*along),
            device_id_type=MESH,
        )

    def landed_part(chunk, half, group, slot, part):
        left, columns = span(chunk, half, part)
        row, column = landing(chunk, half, group, slot)
        return w[row : row + CHIP, column + left : column + left + columns].astype(F32)

    def scatter_begin(chunk, half, groups):
        for group in groups:
            for kind in range(4):
                scatter_copy(chunk, half, group, kind).start()

    def pass_on(chunk, half, group):
        for kind, part, j in ((0, 0, 1), (1, 1, -1)):
            left, columns = span(chunk, half, part)
            scatter_copy(chunk, half, group, kind).wait_recv()
            own = piece(chunk, half, group, j, part)[...].astype(F32)
            total = own + landed_part(chunk, half, group, 0, part)
            passing = (passing_q, passing_u)[chunk]
            left += offset(chunk, half)
            passing[group, :, left : left + columns] = total.astype(BF16)
            scatter_copy(chunk, half, group, 4 + kind).start()

    def finish(chunk, half, group):
        for kind in (2, 3, 4, 5):
            scatter_copy(chunk, half, group, kind).wait_recv()
        for part in (0, 1):
            left, columns = span(chunk, half, part)
            total = (
                piece(chunk, half, group, 0, part)[...].astype(F32)
                + landed_part(chunk, half, group, 1, part)
                + landed_part(chunk, half, group, 2, part)
            )
            if group == 4:
                left = SCATTERED[chunk][half][0] + left
                reduced[:, left : left + columns] = total
            else:
                left += offset(chunk, half)
                sums_of(chunk)[group, :, left : left + columns] = total.astype(BF16)

    def scatter_sent(chunk):
        for half in (0, 1):
            for group in range(5):
                for kind in range(6):
                    scatter_copy(chunk, half, group, kind).wait_send()

    def give_credit(chunk):
        for device in around:
            pl.semaphore_signal(credit.at[chunk], inc=1, device_id=device, device_id_type=MESH)

    def share_copies(chunk):
        theirs = pl.ds(pl.multiple_of((1 - me.c) * OWN, 8), OWN)
        place = pl.ds(pl.multiple_of(me.c * D, 128), D)
        targets = ((other_share, 0),) if chunk == 0 else ((up_share, UP), (down_share, DOWN))
        return [
            pltpu.make_async_remote_copy(
                src_ref=reduced.at[theirs, pl.ds(left, D)],
                dst_ref=target.at[:, place],
                send_sem=core_sems.at[left // D, 0],
                recv_sem=core_sems.at[left // D, 1],
                device_id=me.core(),
                device_id_type=MESH,
            )
            for target, left in targets
        ]

    def share(chunk):
        mine = pl.ds(pl.multiple_of(me.c * OWN, 8), OWN)
        place = pl.ds(pl.multiple_of(me.c * D, 128), D)
        for copy in share_copies(chunk):
            copy.start()
        targets = ((other_share, 0),) if chunk == 0 else ((up_share, UP), (down_share, DOWN))
        for target, left in targets:
            target[:, place] = reduced[mine, left : left + D]

    def scatter_steps(chunk, half):
        def onward(*groups):
            def run():
                for group in groups:
                    pass_on(chunk, half, group)

            return run

        def ending(*groups):
            def run():
                for group in groups:
                    finish(chunk, half, group)
                if len(groups) > 1:
                    scatter_begin(chunk, half, (4,))

            return run

        return [onward(2, 1), onward(3, 0), ending(2, 1, 3), ending(0), onward(4), ending(4)]


    def rows_copies(kind, act):
        origin, source, target = kinds[kind]

        @pl.when(me.s == origin)
        def _():
            place = target.at[pl.ds(pl.multiple_of(me.r * 64 + me.c * ROWS, ROWS), ROWS)]
            for seq, part in UNITS:
                for t in (0, 1):
                    itself = (me.s == part) & (me.c == seq) & (me.t == t)

                    @pl.when(jnp.logical_not(itself))
                    def _():
                        copy = pltpu.make_async_remote_copy(
                            src_ref=source.at[seq, part],
                            dst_ref=place,
                            send_sem=rows_send.at[kind, seq, part, t],
                            recv_sem=rows_recv.at[kind, me.r, me.c],
                            device_id=me.at(part, seq, t),
                            device_id_type=MESH,
                        )
                        if act == "start":
                            copy.start()
                        else:
                            copy.wait_send()

                    if act == "start":

                        @pl.when(itself)
                        def _():
                            place[...] = source[seq, part]

    def rows_arrive(kind):
        origin, source, target = kinds[kind]
        for r, c in quarters:
            itself = (me.s == origin) & (me.c == c) & (me.r == r)

            @pl.when(jnp.logical_not(itself))
            def _():
                pltpu.make_async_remote_copy(
                    src_ref=source.at[0, 0],
                    dst_ref=target.at[pl.ds(r * 64 + c * ROWS, ROWS)],
                    send_sem=rows_send.at[kind, 0, 0, 0],
                    recv_sem=rows_recv.at[kind, r, c],
                    device_id=me.core(),
                    device_id_type=MESH,
                ).wait_recv()


    def small_copies(step):
        rows = (8, 16, 16)[step]
        devices = (
            [me.core(), me.pair(), diagonal],
            [me.away(0, dx) for dx in (1, 2, 3)],
            [me.away(dz, 0) for dz in (1, 2, 3)],
        )[step]
        source = small.at[step, pl.ds(0, rows)]
        return [
            pltpu.make_async_remote_copy(
                src_ref=source,
                dst_ref=small_in.at[step, index, pl.ds(0, rows)],
                send_sem=small_send.at[step, index],
                recv_sem=small_recv.at[step, index],
                device_id=device,
                device_id_type=MESH,
            )
            for index, device in enumerate(devices)
        ]

    def vector_copy():
        return pltpu.make_async_remote_copy(
            src_ref=small.at[3, pl.ds(8, 8)],
            dst_ref=quarter_total.at[me.c],
            send_sem=core_sems.at[3, 0],
            recv_sem=core_sems.at[3, 1],
            device_id=me.core(),
            device_id_type=MESH,
        )

    def small_steps():
        small[0, 0:8, :] = home_sum[...]
        small[0, 8:16, :] = quarter_sum[...]
        for step in range(3):
            copies = small_copies(step)
            for copy in copies:
                copy.start()
            yield
            for copy in copies:
                copy.wait_recv()
            rows = (8, 16, 16)[step]
            total = small[step, 0:rows, :]
            for index in range(3):
                total = total + small_in[step, index, 0:rows, :]
            small[step + 1, 0:rows, :] = total
            if rows == 8:
                small[step + 1, 8:16, :] = small[step, 8:16, :]
        home_total[...] = small[3, 0:8, :]
        quarter_total[me.c] = small[3, 8:16, :]
        vector_copy().start()
        yield
        vector_copy().wait()
        for step in range(3):
            for copy in small_copies(step):
                copy.wait_send()

    counter = {}

    def new_sems(unit):
        index = counter.get(unit, 0)
        counter[unit] = index + 1
        return (sems_s.at[*unit, index], sems_r.at[*unit, index])

    flying = []

    def fly(source, target, unit, device):
        copy = send(source, target, new_sems(unit), device)
        flying.append(copy)
        return copy

    low_lanes = lax.broadcasted_iota(jnp.int32, (128, 640), 1) % 128 < HEAD
    low_half = lax.broadcasted_iota(jnp.int32, (128, 128), 1) < HEAD

    def first_rows(section, whole, rows_in):
        @pl.when(me.s == section)
        def _():
            mine = pl.ds(pl.multiple_of(me.r * 64 + me.c * ROWS, ROWS), ROWS)
            theirs = pl.ds(pl.multiple_of(me.r * 64 + (1 - me.c) * ROWS, ROWS), ROWS)
            for part in (0, 1):
                sems = (hop_sems.at[0, section, me.c, part], hop_sems.at[1, section, me.c, part])
                copy = send(whole.at[part, theirs], rows_in.at[me.c, part], sems, me.core())
                rows_in[me.c, part] = whole[part, mine, :]
                copy.wait_send()

    def rows_ready(section, rows_in, unit):
        @pl.when(jnp.logical_not((me.s == section) & (me.c == unit[0])))
        def _():
            pltpu.make_async_remote_copy(
                src_ref=rows_in.at[unit],
                dst_ref=rows_in.at[unit],
                send_sem=hop_sems.at[0, section, *unit],
                recv_sem=hop_sems.at[1, section, *unit],
                device_id=me.core(),
                device_id_type=MESH,
            ).wait_recv()

    def hop_copy(section, rows_out, rows_in, unit):
        return pltpu.make_async_remote_copy(
            src_ref=rows_out.at[unit],
            dst_ref=rows_in.at[unit],
            send_sem=hop_sems.at[2, section, *unit],
            recv_sem=hop_sems.at[1, section, *unit],
            device_id=me.other(),
            device_id_type=MESH,
        )

    def spread(rows, unit):
        own = rows.at[*unit, me.r, me.c]
        pair = fly(own, own, unit, me.pair())
        core = fly(own, own, unit, me.core())
        yield
        pair.wait_recv()
        arrived = rows.at[*unit, 1 - me.r, me.c]
        further = fly(arrived, arrived, unit, me.core())
        yield
        core.wait_recv()
        further.wait_recv()

    parts_flying = {}

    def before_part(unit):
        for copy in parts_flying.pop(unit, []):
            copy.wait_send()

    pair_flying = {}

    def collect(which, unit):
        slot = which % 2
        arriving = core_in.at[*unit, slot]
        core = send(part.at[*unit, :, 1 - me.c], arriving, new_sems(unit), me.core())
        parts_flying.setdefault(unit, []).append(core)
        yield
        core.wait_recv()
        theirs = part[*unit, 1 - me.r, me.c].astype(F32) + core_in[*unit, slot, 1 - me.r].astype(F32)
        if (unit, slot) in pair_flying:
            pair_flying[unit, slot].wait_send()
        pair_out[*unit, slot] = theirs.astype(BF16)
        pair = send(pair_out.at[*unit, slot], pair_in.at[*unit, slot], new_sems(unit), me.pair())
        pair_flying[unit, slot] = pair
        mine = part[*unit, me.r, me.c].astype(F32) + core_in[*unit, slot, me.r].astype(F32)
        yield
        pair.wait_recv()
        return mine + pair_in[*unit, slot].astype(F32)

    def norm(rows, which, unit, target):
        centred = rows - jnp.mean(rows, -1, keepdims=True)
        recip = lax.rsqrt(jnp.mean(centred * centred, -1, keepdims=True) + EPS)
        units = centred * recip
        normed[*unit, which] = units
        recips[*unit, which] = recip
        out = units * ln_gain[which : which + 1, :] + ln_bias[which : which + 1, :]
        target[*unit, me.r, me.c] = out.astype(BF16)

    def norm_back(grad, which, unit):
        units = normed[*unit, which]
        scaled = grad * ln_gain[which : which + 1, :]
        inner = (
            scaled
            - jnp.mean(scaled, -1, keepdims=True)
            - units * jnp.mean(scaled * units, -1, keepdims=True)
        )
        home_sum[which : which + 1, :] += jnp.sum(grad * units, 0, keepdims=True)
        home_sum[2 + which : 3 + which, :] += jnp.sum(grad, 0, keepdims=True)
        return inner * recips[*unit, which]

    def tiled(count, body):
        for n in range(count):
            body(n * 256)

    def back_through(rows, left, width, unit):
        def tile(n):
            out = mm_nt(rows, w[pl.ds(n, 256), left : left + width])
            part[*unit, :, :, :, pl.ds(n, 256)] = out.reshape(2, 2, ROWS, 256).astype(BF16)

        tiled(5, tile)

    def causal():
        query = me.z * 128 + lax.broadcasted_iota(jnp.int32, (128, 512), 0)
        key = lax.broadcasted_iota(jnp.int32, (128, 512), 1)
        return key <= query

    def keys_of(unit, head):
        if unit[1] == 0:
            return kv_all[unit[0], head, 0].reshape(512, 128)
        return kv_all[unit[0], head].reshape(1024, 128)


    def first_copy(backwards, unit, index):
        rows = (a_all, g_all)[backwards]
        ref = rows.at[*unit, 1 - me.r if index == 2 else me.r, me.c]
        return pltpu.make_async_remote_copy(
            src_ref=ref,
            dst_ref=ref,
            send_sem=early_sems.at[0, backwards, *unit, index],
            recv_sem=early_sems.at[1, backwards, *unit, index],
            device_id=me.pair() if index == 0 else me.core(),
            device_id_type=MESH,
        )

    def first_start(backwards, unit):
        if backwards:
            rows_ready(1, g_in, unit)
            g_all[*unit, me.r, me.c] = g_in[unit]
        else:
            rows_ready(0, x_in, unit)
            norm(x_in[unit].astype(F32), 0, unit, a_all)
        first_copy(backwards, unit, 0).start()
        first_copy(backwards, unit, 1).start()

    def first_more(backwards, unit):
        first_copy(backwards, unit, 0).wait_recv()
        first_copy(backwards, unit, 2).start()

    def first_end(backwards, unit):
        first_copy(backwards, unit, 1).wait_recv()
        first_copy(backwards, unit, 2).wait_recv()

    def first_spread(backwards, unit):
        first_start(backwards, unit)
        yield
        first_more(backwards, unit)
        yield
        first_end(backwards, unit)

    up, down = (me.away(1, 0), me.away(-1, 0))
    first, second = (pl.ds(0, 64), pl.ds(64, 64))

    def forward(unit, section):
        seq, micro = unit
        probs = (probs_one, probs_two)[micro]
        if section == 1:
            yield from first_spread(0, unit)
        rows = x_in[unit].astype(F32)
        a = a_all[unit].reshape(128, D)
        pairs = (mm(a, w[:, KV:QO]) + biases[me.c, 0:1, KV:QO]).astype(BF16)
        for head in range(HEADS):
            kv_all[seq, head, micro, me.z] = pairs[:, head * 128 : head * 128 + 128]

        def block(place, half):
            return kv_all.at[seq, :, micro, (me.z + place) % 4, half]

        up_first = fly(block(0, first), block(0, first), unit, up)
        down_second = fly(block(0, second), block(0, second), unit, down)
        up_second = fly(block(0, second), block(0, second), unit, up)
        down_first = fly(block(0, first), block(0, first), unit, down)
        queries = jnp.where(low_lanes, mm(a, w[:, QO:UP]) + biases[me.c, 0:1, QO:UP], 0.0)
        queries = (queries.astype(BF16).astype(F32) * HEAD**-0.5).astype(BF16)
        for head in range(HEADS):
            q_pad[*unit, head] = queries[:, head * 128 : head * 128 + 128]
        yield
        up_first.wait_recv()
        far_up = fly(block(3, first), block(3, first), unit, up)
        down_second.wait_recv()
        far_down = fly(block(1, second), block(1, second), unit, down)
        yield
        for copy in (up_second, down_first, far_up, far_down):
            copy.wait_recv()

        def one_head(head):
            pairs = keys_of(unit, head)
            scores = mm_nt(q_pad[*unit, head], pairs)
            recent = jnp.where(causal(), scores[:, -512:], NEG)
            scores = recent if micro == 0 else jnp.concatenate((scores[:, :512], recent), 1)
            weights = jnp.exp(scores - jnp.max(scores, -1, keepdims=True))
            share = 1.0 / jnp.sum(weights, -1, keepdims=True)
            shares[*unit, :, head : head + 1] = share
            weights = weights.astype(BF16)
            probs[seq, head] = weights
            out = jnp.where(low_half, 0.0, mm(weights, pairs) * share)
            o_all[*unit, :, head * 128 : head * 128 + 128] = out.astype(BF16)

        for head in range(HEADS):
            one_head(head)
        back_through(o_all[unit], QO, 640, unit)
        total = yield from collect(0, unit)
        rows = rows + total + branch_bias[0:1, :]
        norm(rows, 1, unit, c_all)
        yield from spread(c_all, unit)

        def up_tile(n):
            columns = pl.ds(n, 256)
            pre = mm(c_all[unit].reshape(128, D), w[:, pl.ds(UP + n, 256)]) + biases[me.c, 1:2, columns]
            scale = 0.7978845608028654
            square = pre * pre
            curve = jnp.tanh(scale * (pre + 0.044715 * (square * pre)))
            half = 0.5 * (1.0 + curve)
            hidden[*unit, :, columns] = (pre * half).astype(BF16)
            slope = half + 0.5 * pre * (1.0 - curve * curve) * (scale * (1.0 + 3 * 0.044715 * square))
            slopes[*unit, :, columns] = slope.astype(BF16)

        tiled(5, up_tile)
        before_part(unit)
        back_through(hidden[unit], DOWN, 1280, unit)
        total = yield from collect(1, unit)
        rows = rows + total + branch_bias[1:2, :]
        out_rows[unit] = rows.astype(BF16)
        if section == 0:
            hop_copy(0, out_rows, x_in, unit).start()

    def backward(unit, section):
        seq, micro = unit
        probs = (probs_one, probs_two)[micro]
        if section == 0:
            yield from first_spread(1, unit)
        rows = g_in[unit].astype(F32)
        home_sum[5:6, :] += jnp.sum(rows, 0, keepdims=True)

        def down_tile(n):
            columns = pl.ds(n, 256)
            grad = mm(g_all[unit].reshape(128, D), w[:, pl.ds(DOWN + n, 256)])
            grad = (grad * slopes[*unit, :, columns].astype(F32)).astype(BF16)
            du_all[*unit, :, columns] = grad
            quarter_sum[1:2, columns] += jnp.sum(grad.astype(F32), 0, keepdims=True)

        tiled(5, down_tile)
        before_part(unit)
        back_through(du_all[unit], UP, 1280, unit)
        total = yield from collect(2, unit)
        rows = rows + norm_back(total, 1, unit)
        low = rows.astype(BF16)
        ga_all[*unit, me.r, me.c] = low
        home_sum[4:5, :] += jnp.sum(low.astype(F32), 0, keepdims=True)
        yield from spread(ga_all, unit)
        grad = mm(ga_all[unit].reshape(128, D), w[:, QO:UP])
        go_pad[unit] = jnp.where(low_lanes, 0.0, grad).astype(BF16)

        def one_head(head):
            pairs = keys_of(unit, head)
            columns = pl.ds(head * 128, 128)
            out_grads = (go_pad[*unit, :, columns].astype(F32) * shares[*unit, :, head : head + 1]).astype(BF16)
            queries = q_pad[*unit, head]
            low = probs[seq, head]
            pulled = low.astype(F32) * mm_nt(out_grads, pairs)
            delta = shares[*unit, :, head : head + 1] * jnp.sum(pulled, -1, keepdims=True)
            grad = (pulled - low.astype(F32) * delta).astype(BF16)
            query_grad = mm(grad, pairs) * HEAD**-0.5
            place = pl.ds(QO + head * 128, 128)
            dqkv[*unit, :, place] = jnp.where(low_half, query_grad, 0.0).astype(BF16)
            pairs_grad = mm_tn(grad, queries) + mm_tn(low, out_grads)
            if micro == 1:
                pairs_grad = pairs_grad.reshape(2, 4, 128, 128)
                dkv_part[seq, head, 0] = pairs_grad[0].astype(BF16)
                dkv_part[seq, head, 1] = pairs_grad[1].astype(BF16)
            else:
                total = dkv_part[seq, head, 0].astype(F32) + pairs_grad.reshape(4, 128, 128)
                dkv_part[seq, head, 0] = total.astype(BF16)

        for head in range(HEADS):
            one_head(head)
        far, right, left = ((me.z + 2) % 4, (me.z + 1) % 4, (me.z + 3) % 4)

        def block(place, half):
            return dkv_part.at[seq, :, micro, place, half]

        def land(slot, half):
            return dkv_in.at[*unit, slot, :, half]

        far_up = fly(block(far, first), land(0, first), unit, up)
        far_down = fly(block(far, second), land(0, second), unit, down)
        up_own = fly(block(right, second), land(1, second), unit, up)
        down_own = fly(block(left, first), land(2, first), unit, down)
        yield
        far_up.wait_recv()
        total = dkv_part[seq, :, micro, right, 0:64].astype(F32) + dkv_in[*unit, 0, :, 0:64].astype(F32)
        dkv_in[*unit, 0, :, 0:64] = total.astype(BF16)
        up_sum = fly(land(0, first), land(1, first), unit, up)
        far_down.wait_recv()
        total = dkv_part[seq, :, micro, left, 64:128].astype(F32) + dkv_in[*unit, 0, :, 64:128].astype(F32)
        dkv_in[*unit, 0, :, 64:128] = total.astype(BF16)
        down_sum = fly(land(0, second), land(2, second), unit, down)
        yield
        for copy in (up_own, down_own, up_sum, down_sum):
            copy.wait_recv()
        for head in range(HEADS):
            total = dkv_part[seq, head, micro, me.z].astype(F32)
            for slot in (1, 2):
                total = total + dkv_in[*unit, slot, head].astype(F32)
            dqkv[*unit, :, head * 128 : head * 128 + 128] = total.astype(BF16)
        before_part(unit)
        back_through(dqkv[unit], KV, 1280, unit)
        total = yield from collect(3, unit)
        rows = rows + norm_back(total, 0, unit)
        grad_rows[unit] = rows.astype(BF16)
        if section == 1:
            hop_copy(1, grad_rows, g_in, unit).start()

    def grad_wide(rows, other, left):
        def tile(n):
            out = mm_tn(rows[...].reshape(512, D), other[:, :, :, pl.ds(n, 256)].reshape(512, 256))
            grads[:, pl.ds(left + n, 256)] = out.astype(BF16)

        tiled(5, tile)

    def grad_narrow(rows, other, begin, left, more):
        def tile(n):
            place = pl.ds(n, 256)
            turned = rows[:, :, :, :, :, place].reshape(512, 256)
            out = mm_tn(turned, other[:, :, :, begin : begin + 640].reshape(512, 640))
            if more:
                out = out + grads[place, left : left + 640].astype(F32)
            grads[place, left : left + 640] = out.astype(BF16)

        tiled(5, tile)

    home_sum[...] = jnp.zeros_like(home_sum)
    quarter_sum[...] = jnp.zeros_like(quarter_sum)
    none = jnp.zeros((1, HEAD), F32)
    for head in range(2 * HEADS):
        quarter, place = (head // HEADS, head % HEADS * 128)
        columns = slice(head * HEAD, head * HEAD + HEAD)
        pairs = (w_qkv[1, :, columns], w_qkv[2, :, columns])
        others = (w_qkv[0, :, columns], w_out[:, columns])
        for left, two in ((KV, pairs), (QO, others)):
            both = jnp.concatenate([x.astype(F32) for x in two], 1)
            shard[quarter, :, left + place : left + place + 128] = both
        both = jnp.concatenate((none, qv_bias[1:2, columns]), 1)
        biases[quarter, 0:1, KV + place : KV + place + 128] = both
        both = jnp.concatenate((qv_bias[0:1, columns], none), 1)
        biases[quarter, 0:1, QO + place : QO + place + 128] = both
    for quarter in (0, 1):
        columns = slice(quarter * D, quarter * D + D)
        shard[quarter, :, UP:DOWN] = w_up[:, columns].astype(F32)
        shard[quarter, :, DOWN:COLS] = w_down[:, columns].astype(F32)
        biases[quarter, 1:2, :] = up_bias[0:1, columns]
    swap = send(shard.at[1 - me.c], reduced.at[pl.ds(0, OWN)], (core_sems.at[4, 0], core_sems.at[4, 1]), me.core())
    first_rows(0, tokens, x_in)
    first_rows(1, out_grad, g_in)
    swap.wait()
    row = pl.multiple_of((me.z * 4 + me.x) * CHIP, 16)
    for start in range(0, COLS, 640):
        columns = slice(start, start + 640)
        mine = shard[me.c, :, columns]
        theirs = reduced[0:OWN, columns]
        lower = jnp.where(me.c == 0, mine, theirs)
        upper = jnp.where(me.c == 0, theirs, mine)
        w[pl.ds(row, CHIP), columns] = jnp.concatenate((lower, upper), 0).astype(BF16)

    def each(steps):
        for step in steps:
            step()
            yield

    def landed_all():
        for copy in flying + list(pair_flying.values()):
            copy.wait_send()
        for unit in UNITS:
            before_part(unit)
        flying.clear()
        pair_flying.clear()

    def begin(backwards):
        lower, upper = (gather_steps(0, 0), gather_steps(0, 1))
        heavy_z, heavy_x = (gather_steps(1, 0), gather_steps(1, 1))

        def both(*indices):
            for index in indices:
                lower[index]()
                upper[index]()

        both(0, 1)
        for unit in UNITS:
            first_start(backwards, unit)
        both(2, 3, 4)
        heavy_x[0]()
        heavy_z[0]()
        for unit in UNITS:
            first_more(backwards, unit)
        both(5, 6, 7, 8)
        for unit in UNITS:
            first_end(backwards, unit)
        return [
            heavy_x[1:3],
            heavy_x[3:5],
            heavy_z[1:3],
            heavy_x[5:7],
            heavy_z[3:5],
            heavy_x[7:8] + heavy_z[5:6],
            heavy_z[6:8],
            heavy_x[8:] + heavy_z[8:],
        ]

    def scatter_down():
        give_credit(1)
        grad_wide(g_all, hidden, DOWN)

    def scatter_up():
        grad_wide(c_all, du_all, UP)
        pl.semaphore_wait(credit.at[1], 4)
        scatter_begin(1, 1, (2, 1, 3, 0))

    def scatter_parts():
        lower, upper = (scatter_steps(1, 1), scatter_steps(1, 0))
        return [
            [scatter_down],
            [scatter_up],
            [lambda: scatter_begin(1, 0, (2, 1, 3, 0)), lambda: grad_narrow(ga_all, o_all, 0, QO, False)],
            lower[0:2],
            lower[2:4],
            upper[0:2],
            lower[4:5],
            upper[2:4],
            lower[5:] + upper[4:5],
            upper[5:] + [lambda: share(1)],
        ]

    def run(steps):
        for step in steps:
            step()


    def scatter_last(waiting):
        waiting = iter(waiting)

        def earlier():
            run(next(waiting, []))

        smalls = small_steps()
        give_credit(0)
        grad_narrow(a_all, dqkv, QO, QO, True)
        column_sum = jnp.sum(dqkv[...].astype(F32), axis=(0, 1, 2))
        quarter_sum[0:1, :] += column_sum.reshape(1, D)
        next(smalls, None)
        grad_narrow(a_all, dqkv, KV, KV, False)
        pl.semaphore_wait(credit.at[0], 4)
        scatter_begin(0, 1, (2, 1, 3, 0))
        scatter_begin(0, 0, (2, 1, 3, 0))
        lower, upper = (scatter_steps(0, 1), scatter_steps(0, 0))
        earlier()
        next(smalls, None)
        earlier()
        run(lower[0:2])
        next(smalls, None)
        run(upper[0:2])
        earlier()
        run(lower[2:4])
        next(smalls, None)
        earlier()
        run(upper[2:4])
        next(smalls, None)
        earlier()
        run(lower[4:5] + upper[4:5])
        earlier()
        run(lower[5:] + upper[5:])
        share(0)

    @pl.when(me.s == 0)
    def _():
        stages = dict(zip("ABCD", [forward(unit, 0) for unit in UNITS]))
        steps = each([functools.partial(run, steps) for steps in begin(0)])
        stages.update(dict.fromkeys("01234567", steps))
        in_order(FIRST_FORWARD, stages)
        landed_all()
        for unit in UNITS:
            hop_copy(0, out_rows, x_in, unit).wait_send()

    @pl.when(me.s == 1)
    def _():
        for steps in begin(1):
            run(steps)
        counter.clear()
        stages = dict(zip("ABCD", [forward(unit, 1) for unit in UNITS]))
        stages.update(zip("abcd", [backward(unit, 1) for unit in UNITS[2:] + UNITS[:2]]))
        in_order("".join(LAST_PASSES), stages)
        landed_all()

    rows_copies(0, "start")

    @pl.when(me.s == 1)
    def _():
        for unit in UNITS:
            hop_copy(1, grad_rows, g_in, unit).wait_send()
        steps = scatter_parts()
        for part in steps[:4]:
            run(part)
        scatter_last(steps[4:])

    @pl.when(me.s == 0)
    def _():
        for unit in UNITS:
            counter[unit] = 16
        stages = dict(zip("ABCD", [backward(unit, 0) for unit in UNITS[2:] + UNITS[:2]]))
        steps = scatter_parts()
        stages.update(dict.fromkeys("0123", each([functools.partial(run, part) for part in steps[:4]])))
        in_order(FIRST_BACKWARD, stages)
        landed_all()
        rows_copies(1, "start")
        scatter_last(steps[4:])

    rows_arrive(0)
    rows_arrive(1)
    for copy in share_copies(0) + share_copies(1):
        copy.wait()
    scatter_sent(0)
    scatter_sent(1)
    for unit in UNITS:
        for index in range(3):
            first_copy(0, unit, index).wait_send()
            first_copy(1, unit, index).wait_send()
    rows_copies(0, "wait")
    rows_copies(1, "wait")


def lower_of(block):
    return block[:, :HEAD]


def upper_of(block):
    return block[:, HEAD:]


def unpack_kernel(
    other_share,
    home_total,
    quarter_total,
    up_share,
    down_share,
    out_block,
    grad_block,
    qkv_grad,
    out_grad,
    gain_grad,
    bias_grad,
    qv_grad,
    branch_grad,
    up_bias_grad,
    up_grad,
    down_grad,
    out_final,
    grad_final,
    sems,
):
    moved = ((up_share, up_grad), (down_share, down_grad), (out_block, out_final), (grad_block, grad_final))
    copies = [pltpu.make_async_copy(a, b, sems.at[n]) for n, (a, b) in enumerate(moved)]
    for copy in copies:
        copy.start()

    def blocks(rows, left):
        return [rows(head // HEADS, left + head % HEADS * 128) for head in range(2 * HEADS)]

    def of_share(quarter, column):
        return other_share[:, quarter * D + column : quarter * D + column + 128]

    def of_sums(quarter, column):
        return quarter_total[quarter, 0:1, column : column + 128]

    pairs, others = (blocks(of_share, KV), blocks(of_share, QO))
    for n in range(HEADS):
        columns = slice(n * 128, n * 128 + 128)
        two = slice(2 * n, 2 * n + 2)
        qkv_grad[0, :, columns] = jnp.concatenate([lower_of(x) for x in others[two]], 1)
        qkv_grad[1, :, columns] = jnp.concatenate([lower_of(x) for x in pairs[two]], 1)
        qkv_grad[2, :, columns] = jnp.concatenate([upper_of(x) for x in pairs[two]], 1)
        out_grad[:, columns] = jnp.concatenate([upper_of(x) for x in others[two]], 1)
    pairs, others = (blocks(of_sums, KV), blocks(of_sums, QO))
    for n in range(HEADS):
        columns = slice(n * 128, n * 128 + 128)
        two = slice(2 * n, 2 * n + 2)
        qv_grad[0:1, columns] = jnp.concatenate([lower_of(x) for x in others[two]], 1)
        qv_grad[1:2, columns] = jnp.concatenate([upper_of(x) for x in pairs[two]], 1)
    gain_grad[...] = home_total[0:2, :]
    bias_grad[...] = home_total[2:4, :]
    branch_grad[...] = home_total[4:6, :]
    for quarter in (0, 1):
        up_bias_grad[0:1, quarter * D : quarter * D + D] = quarter_total[quarter, 1:2, :]
    for copy in copies:
        copy.wait()


def vmem(shape, kind):
    return pltpu.VMEM(shape, kind)


def call(kernel, name, operands, outs, scratch=(), flops=0, kept=0, **params):
    whole = pl.BlockSpec(memory_space=pltpu.VMEM)
    there = [pl.BlockSpec(memory_space=pl.ANY)] * kept
    moved = sum(a.size * a.dtype.itemsize for a in operands)
    return pl.pallas_call(
        kernel,
        name=name,
        out_shape=[jax.ShapeDtypeStruct(shape, kind) for shape, kind in outs],
        in_specs=[whole] * (len(operands) - kept) + there,
        out_specs=[whole] * (len(outs) - kept) + there,
        scratch_shapes=scratch,
        cost_estimate=pl.CostEstimate(flops=flops, bytes_accessed=moved, transcendentals=0),
        compiler_params=pltpu.CompilerParams(**params),
    )(*operands)


def per_device(
    tokens, ln_gain, ln_bias, w_qkv, qv_bias, w_out, branch_bias, w_up, up_bias, w_down, out_grad
):
    dma = pltpu.SemaphoreType.DMA
    up_share, down_share, other_share, home_total, quarter_total, out_block, grad_block = call(
        layers_kernel,
        "layers",
        [
            tokens[0],
            out_grad[0],
            w_qkv[0].transpose(1, 0, 2),
            w_out[0].T,
            w_up[0],
            w_down[0].T,
            qv_bias[0],
            up_bias,
            ln_gain[0],
            ln_bias[0],
            branch_bias[0],
        ],
        [
            ((OWN, 2 * D), F32),
            ((OWN, 2 * D), F32),
            ((OWN, 2 * D), F32),
            ((8, D), F32),
            ((2, 8, D), F32),
            ((128, D), BF16),
            ((128, D), BF16),
        ],
        [
            vmem((2, OWN, COLS), F32),
            vmem((2, 2, D), F32),
            vmem((D, COLS), BF16),
            vmem((2, 2, ROWS, D), BF16),
            vmem((2, 2, ROWS, D), BF16),
            vmem((2, 2, ROWS, D), BF16),
            vmem((2, 2, ROWS, D), BF16),
            vmem((2, 2, 2, 2, ROWS, D), BF16),
            vmem((2, 2, 2, 2, ROWS, D), BF16),
            vmem((2, 2, 2, 2, ROWS, D), BF16),
            vmem((2, 2, 2, 2, ROWS, D), BF16),
            vmem((2, 2, HEADS, 128, 128), BF16),
            vmem((2, HEADS, 2, 4, 128, 128), BF16),
            vmem((2, HEADS, 128, 512), BF16),
            vmem((2, HEADS, 128, 1024), BF16),
            vmem((2, 2, 128, 640), BF16),
            vmem((2, 2, 128, D), BF16),
            vmem((2, 2, 128, D), BF16),
            vmem((2, 2, 128, D), BF16),
            vmem((2, 2, 128, 640), BF16),
            vmem((2, 2, 128, D), BF16),
            vmem((2, HEADS, 2, 4, 128, 128), BF16),
            vmem((2, 2, 3, HEADS, 128, 128), BF16),
            vmem((2, 2, 2, 2, ROWS, D), BF16),
            vmem((2, 2, 2, 2, ROWS, D), BF16),
            vmem((2, 2, 2, ROWS, D), BF16),
            vmem((2, 2, 2, ROWS, D), BF16),
            vmem((2, 2, 2, ROWS, D), F32),
            vmem((2, 2, 2, ROWS, 1), F32),
            vmem((2, 2, 128, 128), F32),
            vmem((D, COLS), BF16),
            vmem((5, CHIP, 1280), BF16),
            vmem((5, CHIP, 2560), BF16),
            vmem((4, CHIP, 1280), BF16),
            vmem((4, CHIP, 2560), BF16),
            vmem((CHIP, COLS), F32),
            vmem((8, D), F32),
            vmem((8, D), F32),
            vmem((4, 16, D), F32),
            vmem((3, 3, 16, D), F32),
            dma((2, 2, 32)),
            dma((2, 2, 32)),
            dma((3, 2, 2, 2)),
            dma((2, 2, 2, 2, 3)),
            dma((2, 2, 5, 4)),
            dma((2, 2, 5, 4)),
            dma((2, 2, 5, 6)),
            dma((2, 2, 5, 6)),
            dma((5, 2)),
            dma((3, 3)),
            dma((3, 3)),
            dma((2, 2, 2, 2)),
            dma((2, 2, 2)),
            pltpu.SemaphoreType.REGULAR((2,)),
        ],
        2 * 512 * D * COLS * 3,
        collective_id=0,
        has_side_effects=True,
        vmem_limit_bytes=64 * MIB,
    )
    results = call(
        unpack_kernel,
        "unpack",
        [other_share, home_total, quarter_total, up_share, down_share, out_block, grad_block],
        [
            ((3, OWN, 640), F32),
            ((OWN, 640), F32),
            ((2, D), F32),
            ((2, D), F32),
            ((2, 640), F32),
            ((2, D), F32),
            ((1, 2 * D), F32),
            ((OWN, 2 * D), F32),
            ((OWN, 2 * D), F32),
            ((128, D), BF16),
            ((128, D), BF16),
        ],
        [dma((4,))],
        kept=4,
        vmem_limit_bytes=64 * MIB,
    )
    qkv_grad, w_out_grad, gain_grad, bias_grad, qv_grad, branch_grad = results[:6]
    up_bias_grad, up_grad, down_grad, out_final, grad_final = results[6:]
    return (
        out_final[None, None],
        grad_final[None, None],
        gain_grad[None],
        bias_grad[None],
        qkv_grad.transpose(1, 0, 2)[None],
        qv_grad[None],
        w_out_grad.T[None],
        branch_grad[None],
        up_grad[None],
        up_bias_grad,
        down_grad.T[None],
    )


def solution(mesh):
    weights = P("section", ("ctx", "dp"), None, "tp")
    up = P("section", ("ctx", "dp"), "tp")
    down = P("section", "tp", ("ctx", "dp"))
    vector = P("section", None, None)
    return jax.shard_map(
        per_device,
        mesh=mesh,
        in_specs=(
            P("dp", None, "ctx", None),
            vector,
            vector,
            weights,
            P("section", None, "tp"),
            down,
            vector,
            up,
            P("section", "tp"),
            down,
            P("dp", None, "ctx", None),
        ),
        out_specs=(
            P("dp", "section", "ctx", None),
            P("dp", "section", "ctx", None),
            vector,
            vector,
            weights,
            P("section", None, "tp"),
            down,
            vector,
            up,
            P("section", "tp"),
            down,
        ),
        check_vma=False,
    )
```

```python
import functools

import jax
import jax.numpy as jnp
from jax import lax
from jax.experimental import pallas as pl
from jax.experimental.pallas import tpu as pltpu
from jax.sharding import PartitionSpec as P

MESH = pl.DeviceIdType.MESH
F32 = jnp.float32
BF16 = jnp.bfloat16
D = 1280
HEAD = 64
HEADS = 5
ROWS = 32
UNITS = ((0, 0), (1, 0), (0, 1), (1, 1))
KV, QO, UP, DOWN, COLS = (0, 640, 1280, 2560, 3840)
OWN = 40
CHIP = 80
GATHERED = (((0, 640, 384), (640, 640, 384)), ((1280, 640, 384), (1920, 1920, 1024)))
SCATTERED = (((0, 512, 256), (512, 768, 384)), ((1280, 1024, 512), (2304, 1536, 768)))
FIRST_FORWARD = "0ABCD1ABCDA2B3AC4BD5ACB6DAC7BDCDABCDABCDABCD"
LAST_PASSES = ("ABAABCADBCDBCABCADBCDBCADBCDBACDBCDACDAC", "aDAcaBDbcadcbadcabcbdabdabcdabdabcdcbdcd")
FIRST_BACKWARD = "AABACBADBCABDCAD0BCABD1CBDACBDCDACBD2ABCD3ACBDCD"
EPS = 1e-05
NEG = -1e30
MIB = 2**20


class Place:
    def __init__(self):
        self.s = lax.axis_index("section")
        self.z = lax.axis_index("ctx")
        self.dp = lax.axis_index("dp")
        self.t = lax.axis_index("tp")
        self.x = self.dp // 2
        self.c = self.dp % 2
        self.r = (self.s + self.t) % 2

    def core(self):
        return (self.s, self.z, self.x * 2 + 1 - self.c, self.t)

    def pair(self):
        return (self.s, self.z, self.dp, 1 - self.t)

    def other(self):
        return (1 - self.s, self.z, self.dp, 1 - self.t)

    def away(self, dz, dx):
        return (self.s, (self.z + dz + 4) % 4, (self.x + dx + 4) % 4 * 2 + self.c, self.t)

    def at(self, s, seq, t):
        return (s, self.z, self.x * 2 + seq, t)


def send(source, target, sems, device):
    copy = pltpu.make_async_remote_copy(
        src_ref=source,
        dst_ref=target,
        send_sem=sems[0],
        recv_sem=sems[1],
        device_id=device,
        device_id_type=MESH,
    )
    copy.start()
    return copy


def greet(devices):
    barrier = pltpu.get_barrier_semaphore()
    for device in devices:
        pl.semaphore_signal(barrier, inc=1, device_id=device, device_id_type=MESH)
    return barrier


def in_order(order, stages):
    for name in order:
        next(stages[name], None)
    for stage in stages.values():
        assert next(stage, "end") == "end"


def mm(a, b):
    return lax.dot_general(a, b, (((1,), (0,)), ((), ())), preferred_element_type=F32)


def mm_nt(a, b):
    return lax.dot_general(a, b, (((1,), (1,)), ((), ())), preferred_element_type=F32)


def mm_tn(a, b):
    return lax.dot_general(a, b, (((0,), (0,)), ((), ())), preferred_element_type=F32)


def layers_kernel(
    tokens,
    out_grad,
    w_qkv,
    w_out,
    w_up,
    w_down,
    qv_bias,
    up_bias,
    ln_gain,
    ln_bias,
    branch_bias,
    up_share,
    down_share,
    other_share,
    home_total,
    quarter_total,
    out_block,
    grad_block,
    shard,
    biases,
    w,
    x_in,
    g_in,
    out_rows,
    grad_rows,
    a_all,
    c_all,
    g_all,
    ga_all,
    q_pad,
    kv_all,
    probs_one,
    probs_two,
    o_all,
    slopes,
    hidden,
    du_all,
    go_pad,
    dqkv,
    dkv_part,
    dkv_in,
    part,
    core_in,
    pair_out,
    pair_in,
    normed,
    recips,
    shares,
    grads,
    passing_q,
    passing_u,
    sums_q,
    sums_u,
    reduced,
    home_sum,
    quarter_sum,
    small,
    small_in,
    sems_s,
    sems_r,
    hop_sems,
    early_sems,
    gather_send,
    gather_recv,
    scatter_send,
    scatter_recv,
    core_sems,
    small_send,
    small_recv,
    rows_send,
    rows_recv,
    credit,
):
    me = Place()
    diagonal = (me.s, me.z, me.x * 2 + 1 - me.c, 1 - me.t)
    around = [me.away(1, 0), me.away(-1, 0), me.away(0, 1), me.away(0, -1)]
    devices = [me.core(), me.pair(), me.other(), me.away(2, 0), me.away(0, 2), diagonal] + around
    barrier = greet(devices)
    kinds = ((1, out_rows, out_block), (0, grad_rows, grad_block))
    quarters = tuple((r, c) for r in (0, 1) for c in (0, 1))
    for origin, _, _ in kinds:
        for r, c in quarters:
            itself = (me.s == origin) & (me.c == c) & (me.r == r)
            device = me.at(origin, c, (r + origin) % 2)

            @pl.when(jnp.logical_not(itself))
            def _():
                pl.semaphore_signal(barrier, inc=1, device_id=device, device_id_type=MESH)

    pl.semaphore_wait(barrier, 10 + 7)


    def gather_copy(chunk, half, group, kind):
        first, width, cut = GATHERED[chunk][half]
        parts = (cut, width - cut)
        i = (0, 0, -1, 1, 2)[group]
        by = (1, -1)[kind % 2]
        hop_from = (0, 0, -1, 1)[kind]
        part = (None, None, 0, 1)[kind]
        i, j = (hop_from, 0) if group == 0 else (i, hop_from)
        dz, dx = (j, i) if half == 0 else (i, j)
        top = ((me.z + dz + 4) % 4 * 4 + (me.x + dx + 4) % 4) * CHIP
        left = first + (cut if part == 1 else 0)
        columns = width if part is None else parts[part]
        ref = w.at[pl.ds(pl.multiple_of(top, 16), CHIP), pl.ds(left, columns)]
        along = (0, by) if (half == 0) == (group == 0) else (by, 0)
        return pltpu.make_async_remote_copy(
            src_ref=ref,
            dst_ref=ref,
            send_sem=gather_send.at[chunk, half, group, kind],
            recv_sem=gather_recv.at[chunk, half, group, kind],
            device_id=me.away(*along),
            device_id_type=MESH,
        )

    def gather_steps(chunk, half):
        def go(group, *kinds):
            for kind in kinds:
                gather_copy(chunk, half, group, kind).start()

        def landed(group, *kinds):
            for kind in kinds:
                gather_copy(chunk, half, group, kind).wait_recv()

        def first_axis():
            landed(0, 0)
            go(0, 2)
            go(2, 0, 1)
            landed(0, 1)
            go(0, 3)
            go(3, 0, 1)

        def turn(group):
            def run():
                landed(group, 0)
                go(group, 2)
                landed(group, 1)
                go(group, 3)

            return run

        def far():
            landed(0, 2, 3)
            go(4, 0, 1)

        def end():
            for group in (1, 2, 3, 4):
                landed(group, 2, 3)
            for group in range(5):
                for kind in range(4):
                    gather_copy(chunk, half, group, kind).wait_send()

        own = [lambda: go(0, 0, 1), lambda: go(1, 0, 1)]
        return own + [first_axis, turn(1), far, turn(2), turn(3), turn(4), end]


    def landing(chunk, half, group, slot):
        index = group * 3 + slot
        return index * CHIP, SCATTERED[chunk][half][0]

    def span(chunk, half, part):
        _, width, cut = SCATTERED[chunk][half]
        return ((0, cut), (cut, width - cut))[part]

    def offset(chunk, half):
        return SCATTERED[chunk][half][0] - SCATTERED[chunk][0][0]

    def sums_of(chunk):
        return (sums_q, sums_u)[chunk]

    def piece(chunk, half, group, j, part):
        left, columns = span(chunk, half, part)
        if group == 4:
            return sums_of(chunk).at[j % 4, :, pl.ds(offset(chunk, half) + left, columns)]
        dz, dx = (j, group) if half == 0 else (group, j)
        top = ((me.z + dz + 4) % 4 * 4 + (me.x + dx + 4) % 4) * CHIP
        place = pl.ds(SCATTERED[chunk][half][0] + left, columns)
        return grads.at[pl.ds(pl.multiple_of(top, 16), CHIP), place]

    def scatter_copy(chunk, half, group, kind):
        part = (0, 1, 1, 0, 0, 1)[kind]
        slot = (0, 0, 1, 2, 1, 2)[kind]
        by = (1, -1)[kind % 2]
        left, columns = span(chunk, half, part)
        if kind < 4:
            source = piece(chunk, half, group, (2, 2, 1, -1)[kind], part)
        else:
            passing = (passing_q, passing_u)[chunk]
            source = passing.at[group, :, pl.ds(offset(chunk, half) + left, columns)]
        row, column = landing(chunk, half, group, slot)
        along = (by, 0) if (half == 0) == (group != 4) else (0, by)
        return pltpu.make_async_remote_copy(
            src_ref=source,
            dst_ref=w.at[pl.ds(row, CHIP), pl.ds(column + left, columns)],
            send_sem=scatter_send.at[chunk, half, group, kind],
            recv_sem=scatter_recv.at[chunk, half, group, kind],
            device_id=me.away(*along),
            device_id_type=MESH,
        )

    def landed_part(chunk, half, group, slot, part):
        left, columns = span(chunk, half, part)
        row, column = landing(chunk, half, group, slot)
        return w[row : row + CHIP, column + left : column + left + columns].astype(F32)

    def scatter_begin(chunk, half, groups):
        for group in groups:
            for kind in range(4):
                scatter_copy(chunk, half, group, kind).start()

    def pass_on(chunk, half, group):
        for kind, part, j in ((0, 0, 1), (1, 1, -1)):
            left, columns = span(chunk, half, part)
            scatter_copy(chunk, half, group, kind).wait_recv()
            own = piece(chunk, half, group, j, part)[...].astype(F32)
            total = own + landed_part(chunk, half, group, 0, part)
            passing = (passing_q, passing_u)[chunk]
            left += offset(chunk, half)
            passing[group, :, left : left + columns] = total.astype(BF16)
            scatter_copy(chunk, half, group, 4 + kind).start()

    def finish(chunk, half, group):
        for kind in (2, 3, 4, 5):
            scatter_copy(chunk, half, group, kind).wait_recv()
        for part in (0, 1):
            left, columns = span(chunk, half, part)
            total = (
                piece(chunk, half, group, 0, part)[...].astype(F32)
                + landed_part(chunk, half, group, 1, part)
                + landed_part(chunk, half, group, 2, part)
            )
            if group == 4:
                left = SCATTERED[chunk][half][0] + left
                reduced[:, left : left + columns] = total
            else:
                left += offset(chunk, half)
                sums_of(chunk)[group, :, left : left + columns] = total.astype(BF16)

    def scatter_sent(chunk):
        for half in (0, 1):
            for group in range(5):
                for kind in range(6):
                    scatter_copy(chunk, half, group, kind).wait_send()

    def give_credit(chunk):
        for device in around:
            pl.semaphore_signal(credit.at[chunk], inc=1, device_id=device, device_id_type=MESH)

    def share_copies(chunk):
        theirs = pl.ds(pl.multiple_of((1 - me.c) * OWN, 8), OWN)
        place = pl.ds(pl.multiple_of(me.c * D, 128), D)
        targets = ((other_share, 0),) if chunk == 0 else ((up_share, UP), (down_share, DOWN))
        return [
            pltpu.make_async_remote_copy(
                src_ref=reduced.at[theirs, pl.ds(left, D)],
                dst_ref=target.at[:, place],
                send_sem=core_sems.at[left // D, 0],
                recv_sem=core_sems.at[left // D, 1],
                device_id=me.core(),
                device_id_type=MESH,
            )
            for target, left in targets
        ]

    def share(chunk):
        mine = pl.ds(pl.multiple_of(me.c * OWN, 8), OWN)
        place = pl.ds(pl.multiple_of(me.c * D, 128), D)
        for copy in share_copies(chunk):
            copy.start()
        targets = ((other_share, 0),) if chunk == 0 else ((up_share, UP), (down_share, DOWN))
        for target, left in targets:
            target[:, place] = reduced[mine, left : left + D]

    def scatter_steps(chunk, half):
        def onward(*groups):
            def run():
                for group in groups:
                    pass_on(chunk, half, group)

            return run

        def ending(*groups):
            def run():
                for group in groups:
                    finish(chunk, half, group)
                if len(groups) > 1:
                    scatter_begin(chunk, half, (4,))

            return run

        return [onward(2, 1), onward(3, 0), ending(2, 1, 3), ending(0), onward(4), ending(4)]


    def rows_copies(kind, act):
        origin, source, target = kinds[kind]

        @pl.when(me.s == origin)
        def _():
            place = target.at[pl.ds(pl.multiple_of(me.r * 64 + me.c * ROWS, ROWS), ROWS)]
            for seq, part in UNITS:
                for t in (0, 1):
                    itself = (me.s == part) & (me.c == seq) & (me.t == t)

                    @pl.when(jnp.logical_not(itself))
                    def _():
                        copy = pltpu.make_async_remote_copy(
                            src_ref=source.at[seq, part],
                            dst_ref=place,
                            send_sem=rows_send.at[kind, seq, part, t],
                            recv_sem=rows_recv.at[kind, me.r, me.c],
                            device_id=me.at(part, seq, t),
                            device_id_type=MESH,
                        )
                        if act == "start":
                            copy.start()
                        else:
                            copy.wait_send()

                    if act == "start":

                        @pl.when(itself)
                        def _():
                            place[...] = source[seq, part]

    def rows_arrive(kind):
        origin, source, target = kinds[kind]
        for r, c in quarters:
            itself = (me.s == origin) & (me.c == c) & (me.r == r)

            @pl.when(jnp.logical_not(itself))
            def _():
                pltpu.make_async_remote_copy(
                    src_ref=source.at[0, 0],
                    dst_ref=target.at[pl.ds(r * 64 + c * ROWS, ROWS)],
                    send_sem=rows_send.at[kind, 0, 0, 0],
                    recv_sem=rows_recv.at[kind, r, c],
                    device_id=me.core(),
                    device_id_type=MESH,
                ).wait_recv()


    def small_copies(step):
        rows = (8, 16, 16)[step]
        devices = (
            [me.core(), me.pair(), diagonal],
            [me.away(0, dx) for dx in (1, 2, 3)],
            [me.away(dz, 0) for dz in (1, 2, 3)],
        )[step]
        source = small.at[step, pl.ds(0, rows)]
        return [
            pltpu.make_async_remote_copy(
                src_ref=source,
                dst_ref=small_in.at[step, index, pl.ds(0, rows)],
                send_sem=small_send.at[step, index],
                recv_sem=small_recv.at[step, index],
                device_id=device,
                device_id_type=MESH,
            )
            for index, device in enumerate(devices)
        ]

    def vector_copy():
        return pltpu.make_async_remote_copy(
            src_ref=small.at[3, pl.ds(8, 8)],
            dst_ref=quarter_total.at[me.c],
            send_sem=core_sems.at[3, 0],
            recv_sem=core_sems.at[3, 1],
            device_id=me.core(),
            device_id_type=MESH,
        )

    def small_steps():
        small[0, 0:8, :] = home_sum[...]
        small[0, 8:16, :] = quarter_sum[...]
        for step in range(3):
            copies = small_copies(step)
            for copy in copies:
                copy.start()
            yield
            for copy in copies:
                copy.wait_recv()
            rows = (8, 16, 16)[step]
            total = small[step, 0:rows, :]
            for index in range(3):
                total = total + small_in[step, index, 0:rows, :]
            small[step + 1, 0:rows, :] = total
            if rows == 8:
                small[step + 1, 8:16, :] = small[step, 8:16, :]
        home_total[...] = small[3, 0:8, :]
        quarter_total[me.c] = small[3, 8:16, :]
        vector_copy().start()
        yield
        vector_copy().wait()
        for step in range(3):
            for copy in small_copies(step):
                copy.wait_send()

    counter = {}

    def new_sems(unit):
        index = counter.get(unit, 0)
        counter[unit] = index + 1
        return (sems_s.at[*unit, index], sems_r.at[*unit, index])

    flying = []

    def fly(source, target, unit, device):
        copy = send(source, target, new_sems(unit), device)
        flying.append(copy)
        return copy

    low_lanes = lax.broadcasted_iota(jnp.int32, (128, 640), 1) % 128 < HEAD
    low_half = lax.broadcasted_iota(jnp.int32, (128, 128), 1) < HEAD

    def first_rows(section, whole, rows_in):
        @pl.when(me.s == section)
        def _():
            mine = pl.ds(pl.multiple_of(me.r * 64 + me.c * ROWS, ROWS), ROWS)
            theirs = pl.ds(pl.multiple_of(me.r * 64 + (1 - me.c) * ROWS, ROWS), ROWS)
            for part in (0, 1):
                sems = (hop_sems.at[0, section, me.c, part], hop_sems.at[1, section, me.c, part])
                copy = send(whole.at[part, theirs], rows_in.at[me.c, part], sems, me.core())
                rows_in[me.c, part] = whole[part, mine, :]
                copy.wait_send()

    def rows_ready(section, rows_in, unit):
        @pl.when(jnp.logical_not((me.s == section) & (me.c == unit[0])))
        def _():
            pltpu.make_async_remote_copy(
                src_ref=rows_in.at[unit],
                dst_ref=rows_in.at[unit],
                send_sem=hop_sems.at[0, section, *unit],
                recv_sem=hop_sems.at[1, section, *unit],
                device_id=me.core(),
                device_id_type=MESH,
            ).wait_recv()

    def hop_copy(section, rows_out, rows_in, unit):
        return pltpu.make_async_remote_copy(
            src_ref=rows_out.at[unit],
            dst_ref=rows_in.at[unit],
            send_sem=hop_sems.at[2, section, *unit],
            recv_sem=hop_sems.at[1, section, *unit],
            device_id=me.other(),
            device_id_type=MESH,
        )

    def spread(rows, unit):
        own = rows.at[*unit, me.r, me.c]
        pair = fly(own, own, unit, me.pair())
        core = fly(own, own, unit, me.core())
        yield
        pair.wait_recv()
        arrived = rows.at[*unit, 1 - me.r, me.c]
        further = fly(arrived, arrived, unit, me.core())
        yield
        core.wait_recv()
        further.wait_recv()

    parts_flying = {}

    def before_part(unit):
        for copy in parts_flying.pop(unit, []):
            copy.wait_send()

    pair_flying = {}

    def collect(which, unit):
        slot = which % 2
        arriving = core_in.at[*unit, slot]
        core = send(part.at[*unit, :, 1 - me.c], arriving, new_sems(unit), me.core())
        parts_flying.setdefault(unit, []).append(core)
        yield
        core.wait_recv()
        theirs = part[*unit, 1 - me.r, me.c].astype(F32) + core_in[*unit, slot, 1 - me.r].astype(F32)
        if (unit, slot) in pair_flying:
            pair_flying[unit, slot].wait_send()
        pair_out[*unit, slot] = theirs.astype(BF16)
        pair = send(pair_out.at[*unit, slot], pair_in.at[*unit, slot], new_sems(unit), me.pair())
        pair_flying[unit, slot] = pair
        mine = part[*unit, me.r, me.c].astype(F32) + core_in[*unit, slot, me.r].astype(F32)
        yield
        pair.wait_recv()
        return mine + pair_in[*unit, slot].astype(F32)

    def norm(rows, which, unit, target):
        centred = rows - jnp.mean(rows, -1, keepdims=True)
        recip = lax.rsqrt(jnp.mean(centred * centred, -1, keepdims=True) + EPS)
        units = centred * recip
        normed[*unit, which] = units
        recips[*unit, which] = recip
        out = units * ln_gain[which : which + 1, :] + ln_bias[which : which + 1, :]
        target[*unit, me.r, me.c] = out.astype(BF16)

    def norm_back(grad, which, unit):
        units = normed[*unit, which]
        scaled = grad * ln_gain[which : which + 1, :]
        inner = (
            scaled
            - jnp.mean(scaled, -1, keepdims=True)
            - units * jnp.mean(scaled * units, -1, keepdims=True)
        )
        home_sum[which : which + 1, :] += jnp.sum(grad * units, 0, keepdims=True)
        home_sum[2 + which : 3 + which, :] += jnp.sum(grad, 0, keepdims=True)
        return inner * recips[*unit, which]

    def tiled(count, body):
        for n in range(count):
            body(n * 256)

    def back_through(rows, left, width, unit):
        def tile(n):
            out = mm_nt(rows, w[pl.ds(n, 256), left : left + width])
            part[*unit, :, :, :, pl.ds(n, 256)] = out.reshape(2, 2, ROWS, 256).astype(BF16)

        tiled(5, tile)

    def causal():
        query = me.z * 128 + lax.broadcasted_iota(jnp.int32, (128, 512), 0)
        key = lax.broadcasted_iota(jnp.int32, (128, 512), 1)
        return key <= query

    def keys_of(unit, head):
        if unit[1] == 0:
            return kv_all[unit[0], head, 0].reshape(512, 128)
        return kv_all[unit[0], head].reshape(1024, 128)


    def first_copy(backwards, unit, index):
        rows = (a_all, g_all)[backwards]
        ref = rows.at[*unit, 1 - me.r if index == 2 else me.r, me.c]
        return pltpu.make_async_remote_copy(
            src_ref=ref,
            dst_ref=ref,
            send_sem=early_sems.at[0, backwards, *unit, index],
            recv_sem=early_sems.at[1, backwards, *unit, index],
            device_id=me.pair() if index == 0 else me.core(),
            device_id_type=MESH,
        )

    def first_start(backwards, unit):
        if backwards:
            rows_ready(1, g_in, unit)
            g_all[*unit, me.r, me.c] = g_in[unit]
        else:
            rows_ready(0, x_in, unit)
            norm(x_in[unit].astype(F32), 0, unit, a_all)
        first_copy(backwards, unit, 0).start()
        first_copy(backwards, unit, 1).start()

    def first_more(backwards, unit):
        first_copy(backwards, unit, 0).wait_recv()
        first_copy(backwards, unit, 2).start()

    def first_end(backwards, unit):
        first_copy(backwards, unit, 1).wait_recv()
        first_copy(backwards, unit, 2).wait_recv()

    def first_spread(backwards, unit):
        first_start(backwards, unit)
        yield
        first_more(backwards, unit)
        yield
        first_end(backwards, unit)

    up, down = (me.away(1, 0), me.away(-1, 0))
    first, second = (pl.ds(0, 64), pl.ds(64, 64))

    def forward(unit, section):
        seq, micro = unit
        probs = (probs_one, probs_two)[micro]
        if section == 1:
            yield from first_spread(0, unit)
        rows = x_in[unit].astype(F32)
        a = a_all[unit].reshape(128, D)
        pairs = (mm(a, w[:, KV:QO]) + biases[me.c, 0:1, KV:QO]).astype(BF16)
        for head in range(HEADS):
            kv_all[seq, head, micro, me.z] = pairs[:, head * 128 : head * 128 + 128]

        def block(place, half):
            return kv_all.at[seq, :, micro, (me.z + place) % 4, half]

        up_first = fly(block(0, first), block(0, first), unit, up)
        down_second = fly(block(0, second), block(0, second), unit, down)
        up_second = fly(block(0, second), block(0, second), unit, up)
        down_first = fly(block(0, first), block(0, first), unit, down)
        queries = jnp.where(low_lanes, mm(a, w[:, QO:UP]) + biases[me.c, 0:1, QO:UP], 0.0)
        queries = (queries.astype(BF16).astype(F32) * HEAD**-0.5).astype(BF16)
        for head in range(HEADS):
            q_pad[*unit, head] = queries[:, head * 128 : head * 128 + 128]
        yield
        up_first.wait_recv()
        far_up = fly(block(3, first), block(3, first), unit, up)
        down_second.wait_recv()
        far_down = fly(block(1, second), block(1, second), unit, down)
        yield
        for copy in (up_second, down_first, far_up, far_down):
            copy.wait_recv()

        def one_head(head):
            pairs = keys_of(unit, head)
            scores = mm_nt(q_pad[*unit, head], pairs)
            recent = jnp.where(causal(), scores[:, -512:], NEG)
            scores = recent if micro == 0 else jnp.concatenate((scores[:, :512], recent), 1)
            weights = jnp.exp(scores - jnp.max(scores, -1, keepdims=True))
            share = 1.0 / jnp.sum(weights, -1, keepdims=True)
            shares[*unit, :, head : head + 1] = share
            weights = weights.astype(BF16)
            probs[seq, head] = weights
            out = jnp.where(low_half, 0.0, mm(weights, pairs) * share)
            o_all[*unit, :, head * 128 : head * 128 + 128] = out.astype(BF16)

        for head in range(HEADS):
            one_head(head)
        back_through(o_all[unit], QO, 640, unit)
        total = yield from collect(0, unit)
        rows = rows + total + branch_bias[0:1, :]
        norm(rows, 1, unit, c_all)
        yield from spread(c_all, unit)

        def up_tile(n):
            columns = pl.ds(n, 256)
            pre = mm(c_all[unit].reshape(128, D), w[:, pl.ds(UP + n, 256)]) + biases[me.c, 1:2, columns]
            scale = 0.7978845608028654
            square = pre * pre
            curve = jnp.tanh(scale * (pre + 0.044715 * (square * pre)))
            half = 0.5 * (1.0 + curve)
            hidden[*unit, :, columns] = (pre * half).astype(BF16)
            slope = half + 0.5 * pre * (1.0 - curve * curve) * (scale * (1.0 + 3 * 0.044715 * square))
            slopes[*unit, :, columns] = slope.astype(BF16)

        tiled(5, up_tile)
        before_part(unit)
        back_through(hidden[unit], DOWN, 1280, unit)
        total = yield from collect(1, unit)
        rows = rows + total + branch_bias[1:2, :]
        out_rows[unit] = rows.astype(BF16)
        if section == 0:
            hop_copy(0, out_rows, x_in, unit).start()

    def backward(unit, section):
        seq, micro = unit
        probs = (probs_one, probs_two)[micro]
        if section == 0:
            yield from first_spread(1, unit)
        rows = g_in[unit].astype(F32)
        home_sum[5:6, :] += jnp.sum(rows, 0, keepdims=True)

        def down_tile(n):
            columns = pl.ds(n, 256)
            grad = mm(g_all[unit].reshape(128, D), w[:, pl.ds(DOWN + n, 256)])
            grad = (grad * slopes[*unit, :, columns].astype(F32)).astype(BF16)
            du_all[*unit, :, columns] = grad
            quarter_sum[1:2, columns] += jnp.sum(grad.astype(F32), 0, keepdims=True)

        tiled(5, down_tile)
        before_part(unit)
        back_through(du_all[unit], UP, 1280, unit)
        total = yield from collect(2, unit)
        rows = rows + norm_back(total, 1, unit)
        low = rows.astype(BF16)
        ga_all[*unit, me.r, me.c] = low
        home_sum[4:5, :] += jnp.sum(low.astype(F32), 0, keepdims=True)
        yield from spread(ga_all, unit)
        grad = mm(ga_all[unit].reshape(128, D), w[:, QO:UP])
        go_pad[unit] = jnp.where(low_lanes, 0.0, grad).astype(BF16)

        def one_head(head):
            pairs = keys_of(unit, head)
            columns = pl.ds(head * 128, 128)
            out_grads = (go_pad[*unit, :, columns].astype(F32) * shares[*unit, :, head : head + 1]).astype(BF16)
            queries = q_pad[*unit, head]
            low = probs[seq, head]
            pulled = low.astype(F32) * mm_nt(out_grads, pairs)
            delta = shares[*unit, :, head : head + 1] * jnp.sum(pulled, -1, keepdims=True)
            grad = (pulled - low.astype(F32) * delta).astype(BF16)
            query_grad = mm(grad, pairs) * HEAD**-0.5
            place = pl.ds(QO + head * 128, 128)
            dqkv[*unit, :, place] = jnp.where(low_half, query_grad, 0.0).astype(BF16)
            pairs_grad = mm_tn(grad, queries) + mm_tn(low, out_grads)
            if micro == 1:
                pairs_grad = pairs_grad.reshape(2, 4, 128, 128)
                dkv_part[seq, head, 0] = pairs_grad[0].astype(BF16)
                dkv_part[seq, head, 1] = pairs_grad[1].astype(BF16)
            else:
                total = dkv_part[seq, head, 0].astype(F32) + pairs_grad.reshape(4, 128, 128)
                dkv_part[seq, head, 0] = total.astype(BF16)

        for head in range(HEADS):
            one_head(head)
        far, right, left = ((me.z + 2) % 4, (me.z + 1) % 4, (me.z + 3) % 4)

        def block(place, half):
            return dkv_part.at[seq, :, micro, place, half]

        def land(slot, half):
            return dkv_in.at[*unit, slot, :, half]

        far_up = fly(block(far, first), land(0, first), unit, up)
        far_down = fly(block(far, second), land(0, second), unit, down)
        up_own = fly(block(right, second), land(1, second), unit, up)
        down_own = fly(block(left, first), land(2, first), unit, down)
        yield
        far_up.wait_recv()
        total = dkv_part[seq, :, micro, right, 0:64].astype(F32) + dkv_in[*unit, 0, :, 0:64].astype(F32)
        dkv_in[*unit, 0, :, 0:64] = total.astype(BF16)
        up_sum = fly(land(0, first), land(1, first), unit, up)
        far_down.wait_recv()
        total = dkv_part[seq, :, micro, left, 64:128].astype(F32) + dkv_in[*unit, 0, :, 64:128].astype(F32)
        dkv_in[*unit, 0, :, 64:128] = total.astype(BF16)
        down_sum = fly(land(0, second), land(2, second), unit, down)
        yield
        for copy in (up_own, down_own, up_sum, down_sum):
            copy.wait_recv()
        for head in range(HEADS):
            total = dkv_part[seq, head, micro, me.z].astype(F32)
            for slot in (1, 2):
                total = total + dkv_in[*unit, slot, head].astype(F32)
            dqkv[*unit, :, head * 128 : head * 128 + 128] = total.astype(BF16)
        before_part(unit)
        back_through(dqkv[unit], KV, 1280, unit)
        total = yield from collect(3, unit)
        rows = rows + norm_back(total, 0, unit)
        grad_rows[unit] = rows.astype(BF16)
        if section == 1:
            hop_copy(1, grad_rows, g_in, unit).start()

    def grad_wide(rows, other, left):
        def tile(n):
            out = mm_tn(rows[...].reshape(512, D), other[:, :, :, pl.ds(n, 256)].reshape(512, 256))
            grads[:, pl.ds(left + n, 256)] = out.astype(BF16)

        tiled(5, tile)

    def grad_narrow(rows, other, begin, left, more):
        def tile(n):
            place = pl.ds(n, 256)
            turned = rows[:, :, :, :, :, place].reshape(512, 256)
            out = mm_tn(turned, other[:, :, :, begin : begin + 640].reshape(512, 640))
            if more:
                out = out + grads[place, left : left + 640].astype(F32)
            grads[place, left : left + 640] = out.astype(BF16)

        tiled(5, tile)

    home_sum[...] = jnp.zeros_like(home_sum)
    quarter_sum[...] = jnp.zeros_like(quarter_sum)
    none = jnp.zeros((1, HEAD), F32)
    for head in range(2 * HEADS):
        quarter, place = (head // HEADS, head % HEADS * 128)
        columns = slice(head * HEAD, head * HEAD + HEAD)
        pairs = (w_qkv[1, :, columns], w_qkv[2, :, columns])
        others = (w_qkv[0, :, columns], w_out[:, columns])
        for left, two in ((KV, pairs), (QO, others)):
            both = jnp.concatenate([x.astype(F32) for x in two], 1)
            shard[quarter, :, left + place : left + place + 128] = both
        both = jnp.concatenate((none, qv_bias[1:2, columns]), 1)
        biases[quarter, 0:1, KV + place : KV + place + 128] = both
        both = jnp.concatenate((qv_bias[0:1, columns], none), 1)
        biases[quarter, 0:1, QO + place : QO + place + 128] = both
    for quarter in (0, 1):
        columns = slice(quarter * D, quarter * D + D)
        shard[quarter, :, UP:DOWN] = w_up[:, columns].astype(F32)
        shard[quarter, :, DOWN:COLS] = w_down[:, columns].astype(F32)
        biases[quarter, 1:2, :] = up_bias[0:1, columns]
    swap = send(shard.at[1 - me.c], reduced.at[pl.ds(0, OWN)], (core_sems.at[4, 0], core_sems.at[4, 1]), me.core())
    first_rows(0, tokens, x_in)
    first_rows(1, out_grad, g_in)
    swap.wait()
    row = pl.multiple_of((me.z * 4 + me.x) * CHIP, 16)
    for start in range(0, COLS, 640):
        columns = slice(start, start + 640)
        mine = shard[me.c, :, columns]
        theirs = reduced[0:OWN, columns]
        lower = jnp.where(me.c == 0, mine, theirs)
        upper = jnp.where(me.c == 0, theirs, mine)
        w[pl.ds(row, CHIP), columns] = jnp.concatenate((lower, upper), 0).astype(BF16)

    def each(steps):
        for step in steps:
            step()
            yield

    def landed_all():
        for copy in flying + list(pair_flying.values()):
            copy.wait_send()
        for unit in UNITS:
            before_part(unit)
        flying.clear()
        pair_flying.clear()

    def begin(backwards):
        lower, upper = (gather_steps(0, 0), gather_steps(0, 1))
        heavy_z, heavy_x = (gather_steps(1, 0), gather_steps(1, 1))

        def both(*indices):
            for index in indices:
                lower[index]()
                upper[index]()

        both(0, 1)
        for unit in UNITS:
            first_start(backwards, unit)
        both(2, 3, 4)
        heavy_x[0]()
        heavy_z[0]()
        for unit in UNITS:
            first_more(backwards, unit)
        both(5, 6, 7, 8)
        for unit in UNITS:
            first_end(backwards, unit)
        return [
            heavy_x[1:3],
            heavy_x[3:5],
            heavy_z[1:3],
            heavy_x[5:7],
            heavy_z[3:5],
            heavy_x[7:8] + heavy_z[5:6],
            heavy_z[6:8],
            heavy_x[8:] + heavy_z[8:],
        ]

    def scatter_down():
        give_credit(1)
        grad_wide(g_all, hidden, DOWN)

    def scatter_up():
        grad_wide(c_all, du_all, UP)
        pl.semaphore_wait(credit.at[1], 4)
        scatter_begin(1, 1, (2, 1, 3, 0))

    def scatter_parts():
        lower, upper = (scatter_steps(1, 1), scatter_steps(1, 0))
        return [
            [scatter_down],
            [scatter_up],
            [lambda: scatter_begin(1, 0, (2, 1, 3, 0)), lambda: grad_narrow(ga_all, o_all, 0, QO, False)],
            lower[0:2],
            lower[2:4],
            upper[0:2],
            lower[4:5],
            upper[2:4],
            lower[5:] + upper[4:5],
            upper[5:] + [lambda: share(1)],
        ]

    def run(steps):
        for step in steps:
            step()


    def scatter_last(waiting):
        waiting = iter(waiting)

        def earlier():
            run(next(waiting, []))

        smalls = small_steps()
        give_credit(0)
        grad_narrow(a_all, dqkv, QO, QO, True)
        column_sum = jnp.sum(dqkv[...].astype(F32), axis=(0, 1, 2))
        quarter_sum[0:1, :] += column_sum.reshape(1, D)
        next(smalls, None)
        grad_narrow(a_all, dqkv, KV, KV, False)
        pl.semaphore_wait(credit.at[0], 4)
        scatter_begin(0, 1, (2, 1, 3, 0))
        scatter_begin(0, 0, (2, 1, 3, 0))
        lower, upper = (scatter_steps(0, 1), scatter_steps(0, 0))
        earlier()
        next(smalls, None)
        earlier()
        run(lower[0:2])
        next(smalls, None)
        run(upper[0:2])
        earlier()
        run(lower[2:4])
        next(smalls, None)
        earlier()
        run(upper[2:4])
        next(smalls, None)
        earlier()
        run(lower[4:5] + upper[4:5])
        earlier()
        run(lower[5:] + upper[5:])
        share(0)

    @pl.when(me.s == 0)
    def _():
        stages = dict(zip("ABCD", [forward(unit, 0) for unit in UNITS]))
        steps = each([functools.partial(run, steps) for steps in begin(0)])
        stages.update(dict.fromkeys("01234567", steps))
        in_order(FIRST_FORWARD, stages)
        landed_all()
        for unit in UNITS:
            hop_copy(0, out_rows, x_in, unit).wait_send()

    @pl.when(me.s == 1)
    def _():
        for steps in begin(1):
            run(steps)
        counter.clear()
        stages = dict(zip("ABCD", [forward(unit, 1) for unit in UNITS]))
        stages.update(zip("abcd", [backward(unit, 1) for unit in UNITS[2:] + UNITS[:2]]))
        in_order("".join(LAST_PASSES), stages)
        landed_all()

    rows_copies(0, "start")

    @pl.when(me.s == 1)
    def _():
        for unit in UNITS:
            hop_copy(1, grad_rows, g_in, unit).wait_send()
        steps = scatter_parts()
        for part in steps[:4]:
            run(part)
        scatter_last(steps[4:])

    @pl.when(me.s == 0)
    def _():
        for unit in UNITS:
            counter[unit] = 16
        stages = dict(zip("ABCD", [backward(unit, 0) for unit in UNITS[2:] + UNITS[:2]]))
        steps = scatter_parts()
        stages.update(dict.fromkeys("0123", each([functools.partial(run, part) for part in steps[:4]])))
        in_order(FIRST_BACKWARD, stages)
        landed_all()
        rows_copies(1, "start")
        scatter_last(steps[4:])

    rows_arrive(0)
    rows_arrive(1)
    for copy in share_copies(0) + share_copies(1):
        copy.wait()
    scatter_sent(0)
    scatter_sent(1)
    for unit in UNITS:
        for index in range(3):
            first_copy(0, unit, index).wait_send()
            first_copy(1, unit, index).wait_send()
    rows_copies(0, "wait")
    rows_copies(1, "wait")


def lower_of(block):
    return block[:, :HEAD]


def upper_of(block):
    return block[:, HEAD:]


def unpack_kernel(
    other_share,
    home_total,
    quarter_total,
    up_share,
    down_share,
    out_block,
    grad_block,
    qkv_grad,
    out_grad,
    gain_grad,
    bias_grad,
    qv_grad,
    branch_grad,
    up_bias_grad,
    up_grad,
    down_grad,
    out_final,
    grad_final,
):
    up_grad[...] = up_share[...]
    down_grad[...] = down_share[...]
    out_final[...] = out_block[...]
    grad_final[...] = grad_block[...]

    def blocks(rows, left):
        return [rows(head // HEADS, left + head % HEADS * 128) for head in range(2 * HEADS)]

    def of_share(quarter, column):
        return other_share[:, quarter * D + column : quarter * D + column + 128]

    def of_sums(quarter, column):
        return quarter_total[quarter, 0:1, column : column + 128]

    pairs, others = (blocks(of_share, KV), blocks(of_share, QO))
    for n in range(HEADS):
        columns = slice(n * 128, n * 128 + 128)
        two = slice(2 * n, 2 * n + 2)
        qkv_grad[0, :, columns] = jnp.concatenate([lower_of(x) for x in others[two]], 1)
        qkv_grad[1, :, columns] = jnp.concatenate([lower_of(x) for x in pairs[two]], 1)
        qkv_grad[2, :, columns] = jnp.concatenate([upper_of(x) for x in pairs[two]], 1)
        out_grad[:, columns] = jnp.concatenate([upper_of(x) for x in others[two]], 1)
    pairs, others = (blocks(of_sums, KV), blocks(of_sums, QO))
    for n in range(HEADS):
        columns = slice(n * 128, n * 128 + 128)
        two = slice(2 * n, 2 * n + 2)
        qv_grad[0:1, columns] = jnp.concatenate([lower_of(x) for x in others[two]], 1)
        qv_grad[1:2, columns] = jnp.concatenate([upper_of(x) for x in pairs[two]], 1)
    gain_grad[...] = home_total[0:2, :]
    bias_grad[...] = home_total[2:4, :]
    branch_grad[...] = home_total[4:6, :]
    for quarter in (0, 1):
        up_bias_grad[0:1, quarter * D : quarter * D + D] = quarter_total[quarter, 1:2, :]


def vmem(shape, kind):
    return pltpu.VMEM(shape, kind)


def call(kernel, name, operands, outs, scratch=(), flops=0, **params):
    whole = pl.BlockSpec(memory_space=pltpu.VMEM)
    moved = sum(a.size * a.dtype.itemsize for a in operands)
    return pl.pallas_call(
        kernel,
        name=name,
        out_shape=[jax.ShapeDtypeStruct(shape, kind) for shape, kind in outs],
        in_specs=[whole] * len(operands),
        out_specs=[whole] * len(outs),
        scratch_shapes=scratch,
        cost_estimate=pl.CostEstimate(flops=flops, bytes_accessed=moved, transcendentals=0),
        compiler_params=pltpu.CompilerParams(**params),
    )(*operands)


def per_device(
    tokens, ln_gain, ln_bias, w_qkv, qv_bias, w_out, branch_bias, w_up, up_bias, w_down, out_grad
):
    dma = pltpu.SemaphoreType.DMA
    up_share, down_share, other_share, home_total, quarter_total, out_block, grad_block = call(
        layers_kernel,
        "layers",
        [
            tokens[0],
            out_grad[0],
            w_qkv[0].transpose(1, 0, 2),
            w_out[0].T,
            w_up[0],
            w_down[0].T,
            qv_bias[0],
            up_bias,
            ln_gain[0],
            ln_bias[0],
            branch_bias[0],
        ],
        [
            ((OWN, 2 * D), F32),
            ((OWN, 2 * D), F32),
            ((OWN, 2 * D), F32),
            ((8, D), F32),
            ((2, 8, D), F32),
            ((128, D), BF16),
            ((128, D), BF16),
        ],
        [
            vmem((2, OWN, COLS), F32),
            vmem((2, 2, D), F32),
            vmem((D, COLS), BF16),
            vmem((2, 2, ROWS, D), BF16),
            vmem((2, 2, ROWS, D), BF16),
            vmem((2, 2, ROWS, D), BF16),
            vmem((2, 2, ROWS, D), BF16),
            vmem((2, 2, 2, 2, ROWS, D), BF16),
            vmem((2, 2, 2, 2, ROWS, D), BF16),
            vmem((2, 2, 2, 2, ROWS, D), BF16),
            vmem((2, 2, 2, 2, ROWS, D), BF16),
            vmem((2, 2, HEADS, 128, 128), BF16),
            vmem((2, HEADS, 2, 4, 128, 128), BF16),
            vmem((2, HEADS, 128, 512), BF16),
            vmem((2, HEADS, 128, 1024), BF16),
            vmem((2, 2, 128, 640), BF16),
            vmem((2, 2, 128, D), BF16),
            vmem((2, 2, 128, D), BF16),
            vmem((2, 2, 128, D), BF16),
            vmem((2, 2, 128, 640), BF16),
            vmem((2, 2, 128, D), BF16),
            vmem((2, HEADS, 2, 4, 128, 128), BF16),
            vmem((2, 2, 3, HEADS, 128, 128), BF16),
            vmem((2, 2, 2, 2, ROWS, D), BF16),
            vmem((2, 2, 2, 2, ROWS, D), BF16),
            vmem((2, 2, 2, ROWS, D), BF16),
            vmem((2, 2, 2, ROWS, D), BF16),
            vmem((2, 2, 2, ROWS, D), F32),
            vmem((2, 2, 2, ROWS, 1), F32),
            vmem((2, 2, 128, 128), F32),
            vmem((D, COLS), BF16),
            vmem((5, CHIP, 1280), BF16),
            vmem((5, CHIP, 2560), BF16),
            vmem((4, CHIP, 1280), BF16),
            vmem((4, CHIP, 2560), BF16),
            vmem((CHIP, COLS), F32),
            vmem((8, D), F32),
            vmem((8, D), F32),
            vmem((4, 16, D), F32),
            vmem((3, 3, 16, D), F32),
            dma((2, 2, 32)),
            dma((2, 2, 32)),
            dma((3, 2, 2, 2)),
            dma((2, 2, 2, 2, 3)),
            dma((2, 2, 5, 4)),
            dma((2, 2, 5, 4)),
            dma((2, 2, 5, 6)),
            dma((2, 2, 5, 6)),
            dma((5, 2)),
            dma((3, 3)),
            dma((3, 3)),
            dma((2, 2, 2, 2)),
            dma((2, 2, 2)),
            pltpu.SemaphoreType.REGULAR((2,)),
        ],
        2 * 512 * D * COLS * 3,
        collective_id=0,
        has_side_effects=True,
        vmem_limit_bytes=64 * MIB,
    )
    results = call(
        unpack_kernel,
        "unpack",
        [other_share, home_total, quarter_total, up_share, down_share, out_block, grad_block],
        [
            ((3, OWN, 640), F32),
            ((OWN, 640), F32),
            ((2, D), F32),
            ((2, D), F32),
            ((2, 640), F32),
            ((2, D), F32),
            ((1, 2 * D), F32),
            ((OWN, 2 * D), F32),
            ((OWN, 2 * D), F32),
            ((128, D), BF16),
            ((128, D), BF16),
        ],
        vmem_limit_bytes=64 * MIB,
    )
    qkv_grad, w_out_grad, gain_grad, bias_grad, qv_grad, branch_grad = results[:6]
    up_bias_grad, up_grad, down_grad, out_final, grad_final = results[6:]
    return (
        out_final[None, None],
        grad_final[None, None],
        gain_grad[None],
        bias_grad[None],
        qkv_grad.transpose(1, 0, 2)[None],
        qv_grad[None],
        w_out_grad.T[None],
        branch_grad[None],
        up_grad[None],
        up_bias_grad,
        down_grad.T[None],
    )


def solution(mesh):
    weights = P("section", ("ctx", "dp"), None, "tp")
    up = P("section", ("ctx", "dp"), "tp")
    down = P("section", "tp", ("ctx", "dp"))
    vector = P("section", None, None)
    return jax.shard_map(
        per_device,
        mesh=mesh,
        in_specs=(
            P("dp", None, "ctx", None),
            vector,
            vector,
            weights,
            P("section", None, "tp"),
            down,
            vector,
            up,
            P("section", "tp"),
            down,
            P("dp", None, "ctx", None),
        ),
        out_specs=(
            P("dp", "section", "ctx", None),
            P("dp", "section", "ctx", None),
            vector,
            vector,
            weights,
            P("section", None, "tp"),
            down,
            vector,
            up,
            P("section", "tp"),
            down,
        ),
        check_vma=False,
    )
```
